1024 devices in a mesh: dp: 16 (over y, core), expert: 64 (over z, x).
Axes of the slice: x: 8, y: 8, z: 8, core: 2. Of those that a mesh axis runs over, the one named last changes fastest.
Arguments:
- tokens: bfloat16 [1024, 7168], P('expert', 'dp'), may hold values from -6 to 6
- routes: int32 [1024, 8], P('expert'), may hold values from 0 to 31, all different within a row; in each aligned block of 16 rows (0 to 15, 16 to 31, ...) at most 8 rows name the same one
- probs: float32 [1024, 8], P('expert'), may hold values from 0.1 to 0.6
- cotangent: bfloat16 [1024, 7168], P('expert', 'dp'), may hold values from -6 to 6
- w_gate_up: bfloat16 [64, 7168, 2, 512], P('expert', 'dp'), may hold values from -0.0625 to 0.0625
- w_down: bfloat16 [64, 512, 7168], P('expert', None, 'dp'), may hold values from -0.1875 to 0.1875
Outputs:
- combined: bfloat16 [1024, 7168], P('expert', 'dp')
- d_tokens: bfloat16 [1024, 7168], P('expert', 'dp')
- grad_gate_up: bfloat16 [64, 7168, 2, 512], P('expert', 'dp')
The draws below stay inside these ranges and needn't reach their ends.
Inputs may be any that keep to these rules, and one draw needn't show every extreme that they name: `routes`: each row names 8 different experts. Within each block of 16 rows (the tokens of one index of expert) no expert is named by more than 8 rows, a bound that some block reaches.
All inputs are finite; a program needn't handle non-finite values.
Results may differ from the reference program's by a relative error of at most 0.035.
Values may be sent and summed in bfloat16 or wider, within the bound.
A program may use at most 32 MiB of HBM per device.

```python
import math
import jax
import jax.numpy as jnp
import numpy as np
from jax import lax

D = 7168
H = 1024
TOK_DEV = 16
CAP = 8
HALF = 512
TOPK = 8
EXPERTS = 32
TOKENS = 1024
N_DP = 16
N_EXPERT = 64


def block_levels(rng, dims, cuts, low, high):
    def one(dim, shards_of):
        steps = jax.random.uniform(jax.random.fold_in(jax.random.fold_in(rng, 6), dim), (shards_of,), jnp.float32, low / len(cuts), high / len(cuts))
        return jnp.repeat(jnp.exp(steps), dims[dim] // shards_of).reshape((-1,) + (1,) * (len(dims) - dim - 1))

    gain = one(*cuts[0])
    for cut in cuts[1:]:
        gain = gain * one(*cut)
    return gain


def assign_block(key, own, number, rows, count, top, limit, skew):
    sequence = jax.random.permutation(key, count)
    heavy_load, ordinary = shares(count, rows * top, limit, skew, True), shares(count, rows * top, limit, skew, False)
    places = jnp.arange(count)

    def named(tallies, rotation):
        used = int((tallies > 0).sum())
        fixed = max(1, used // 4)
        passed = fixed + (places - fixed + rotation * (used - fixed)) % max(1, count - fixed)
        return jnp.zeros((count,), jnp.int32).at[sequence[jnp.where(places < fixed, places, passed)]].set(jnp.asarray(tallies, jnp.int32))

    tallies = jnp.where(number % 4 == 0, named(heavy_load, number // 4), named(ordinary, number - number // 4 - 1))
    mixed = jax.random.permutation(jax.random.fold_in(own, 3), count)
    giver, receiver = mixed[0:count // 2 * 2:2], mixed[1:count // 2 * 2:2]
    slack = jnp.minimum(tallies[giver] - 1, limit - tallies[receiver]) // 2
    slack = jnp.where((giver == sequence[0]) | (receiver == sequence[0]) | (tallies[receiver] == 0), 0, jnp.maximum(slack, 0))
    passed = jax.random.randint(jax.random.fold_in(own, 4), (count // 2,), 0, 1 << 20) % (slack + 1)
    tallies = tallies.at[giver].add(-passed).at[receiver].add(passed)
    labels = jnp.searchsorted(jnp.cumsum(tallies), jnp.arange(rows * top), side="right").astype(jnp.int32)
    table = labels.reshape(top, rows).T
    table = table[jax.random.permutation(jax.random.fold_in(own, 1), rows)]
    rotation = jax.random.randint(jax.random.fold_in(own, 2), (rows, 1), 0, top)
    return jnp.take_along_axis(table, (jnp.arange(top)[None, :] + rotation) % top, axis=1)


def shares(amount, total, bound, lean, full):
    weights = [(1 << 20) // math.isqrt(grade ** lean) + 1 for grade in range(1, amount + 1)]
    largest = bound if full else min(bound, max(-(-total // amount), total * weights[0] // sum(weights)))
    least = 1 if total - largest >= amount - 1 else 0
    counts, spare = [largest] + [least] * (amount - 1), total - largest - least * (amount - 1)
    while spare > 0:
        movable = [i for i in range(1, amount) if counts[i] < largest] or [i for i in range(1, amount) if counts[i] < bound]
        mass, left = sum([weights[i] for i in movable]), spare
        for i in movable:
            more = min(bound - counts[i], max(1, left * weights[i] // mass), spare)
            counts[i] = counts[i] + more
            spare = spare - more
    return np.array(counts)


def scatter_about(own_key, dims, scale, reach, split=(), kind=jnp.bfloat16):
    gain = block_levels(own_key, dims, split, -0.22, 0.18) if split else 1.0
    drawn = jax.random.normal(own_key, dims, jnp.float32) * scale * gain
    return jnp.minimum(jnp.maximum(drawn, -reach), reach).astype(kind)


def setup_inputs(seed: int = 0) -> dict:
    key_list = jax.random.split(jax.random.key(seed), 7)
    tokens = scatter_about(key_list[0], (TOKENS, D), 1.0, 6.0, ((0, 64), (1, 16)))
    routes_keys = jax.random.split(jax.random.fold_in(key_list[1], 1), TOKENS // TOK_DEV)
    routes_turns = jax.random.permutation(jax.random.fold_in(key_list[1], 3), TOKENS // TOK_DEV)
    routes = jax.vmap(lambda own, number: assign_block(jax.random.fold_in(key_list[1], 2), own, number, TOK_DEV, EXPERTS, TOPK, CAP, 2))(routes_keys, routes_turns).reshape((TOKENS, TOPK))
    probs = jnp.clip(0.1 + 0.5 * jax.random.uniform(key_list[2], (TOKENS, TOPK), jnp.float32) ** block_levels(key_list[2], (TOKENS, TOPK), ((0, 64),), -0.2, 0.2), 0.1, 0.6)
    cotangent = scatter_about(key_list[3], (TOKENS, D), 1.0, 6.0, ((0, 64), (1, 16)))
    w_gate_up = scatter_about(key_list[4], (N_EXPERT, D, 2, HALF), D ** -0.5, 0.0625, ((0, 64), (1, 16)))
    w_down = scatter_about(key_list[5], (N_EXPERT, HALF, D), H ** -0.5, 0.1875, ((0, 64), (2, 16)))
    return {"tokens": tokens, "routes": routes, "probs": probs, "cotangent": cotangent, "w_gate_up": w_gate_up, "w_down": w_down}


def rounded_sum(partial_value, axis_index):
    kept = lax.optimization_barrier(partial_value.astype(jnp.bfloat16))
    return jnp.sum(kept.astype(jnp.float32), axis=axis_index)


def half_pass(rows_x, rows_dy, w_gu, w_dn):
    count_rows = rows_x.shape[0]
    span = rows_x.shape[1] // N_DP
    rows_x3 = rows_x.astype(jnp.float32).reshape(count_rows, N_DP, span)
    w_gu4 = w_gu.astype(jnp.float32).reshape(N_DP, span, 2, HALF)
    pre_act = rounded_sum(jnp.einsum("rnd,ndgh->rngh", rows_x3, w_gu4), 1)
    gate_pre = pre_act[:, 0]
    up_pre = pre_act[:, 1]
    sigmoid_g = jax.nn.sigmoid(gate_pre)
    hidden = (gate_pre * sigmoid_g * up_pre).astype(jnp.bfloat16)
    out_y = jnp.dot(hidden, w_dn, preferred_element_type=jnp.float32).astype(jnp.bfloat16)
    rows_dy3 = rows_dy.astype(jnp.float32).reshape(count_rows, N_DP, span)
    w_dn3 = w_dn.astype(jnp.float32).reshape(HALF, N_DP, span)
    d_hidden = rounded_sum(jnp.einsum("rnd,hnd->rnh", rows_dy3, w_dn3), 1)
    d_gate = d_hidden * up_pre * sigmoid_g * (1.0 + gate_pre * (1.0 - sigmoid_g))
    d_up = d_hidden * gate_pre * sigmoid_g
    d_pre = jnp.stack([d_gate, d_up], axis=1).astype(jnp.bfloat16)
    grad_w = jnp.einsum("rd,rgh->dgh", rows_x.astype(jnp.float32), d_pre.astype(jnp.float32)).astype(jnp.bfloat16)
    out_dx = jnp.einsum("rgh,dgh->rd", d_pre.astype(jnp.float32), w_gu.astype(jnp.float32)).astype(jnp.bfloat16)
    return out_y, out_dx, grad_w


def reference(tokens, routes, probs, cotangent, w_gate_up, w_down):
    count = TOKENS * TOPK
    flat_ids = routes.reshape(-1).astype(jnp.int32)
    onehot = (flat_ids[:, None] == jnp.arange(EXPERTS, dtype=jnp.int32)[None, :]).astype(jnp.int32)
    blocks = onehot.reshape(N_EXPERT, TOK_DEV * TOPK, EXPERTS)
    before = (jnp.cumsum(blocks, axis=1) - blocks).reshape(count, EXPERTS)
    slot_rank = jnp.sum(before * onehot, axis=1).astype(jnp.int32)
    route_numbers = jnp.arange(count, dtype=jnp.int32)
    source = (route_numbers // (TOK_DEV * TOPK)).astype(jnp.int32)
    position = (flat_ids * (N_EXPERT * CAP) + source * CAP + slot_rank).astype(jnp.int32)
    table = jnp.full((EXPERTS * N_EXPERT * CAP,), count, jnp.int32).at[position].set(route_numbers)
    table = table.reshape(EXPERTS, N_EXPERT * CAP)
    route_token = (route_numbers // TOPK).astype(jnp.int32)
    token_pad = jnp.concatenate([tokens, jnp.zeros((1, D), jnp.bfloat16)], axis=0)
    route_cot = (probs.reshape(-1)[:, None] * cotangent[route_token].astype(jnp.float32)).astype(jnp.bfloat16)
    cot_pad = jnp.concatenate([route_cot, jnp.zeros((1, D), jnp.bfloat16)], axis=0)
    token_index = jnp.concatenate([route_token, jnp.array([TOKENS], jnp.int32)])
    route_prob = jnp.concatenate([probs.reshape(-1), jnp.zeros((1,), jnp.float32)])

    def per_expert(carry, expert):
        out_sum, grad_sum = carry
        entries = table[expert]
        tok_idx = token_index[entries]
        rows_x = token_pad[tok_idx]
        rows_dy = cot_pad[entries]
        results = []
        for half_idx in range(2):
            which = (2 * expert + half_idx).astype(jnp.int32)
            w_gu = lax.dynamic_index_in_dim(w_gate_up, which, 0, keepdims=False)
            w_dn = lax.dynamic_index_in_dim(w_down, which, 0, keepdims=False)
            results.append(half_pass(rows_x, rows_dy, w_gu, w_dn))
        y_sum = results[0][0].astype(jnp.float32) + results[1][0].astype(jnp.float32)
        dx_sum = results[0][1].astype(jnp.float32) + results[1][1].astype(jnp.float32)
        out_sum = out_sum.at[tok_idx].add(route_prob[entries][:, None] * y_sum)
        grad_sum = grad_sum.at[tok_idx].add(dx_sum)
        return (out_sum, grad_sum), jnp.stack([results[0][2], results[1][2]], axis=0)

    start = (jnp.zeros((TOKENS + 1, D), jnp.float32), jnp.zeros((TOKENS + 1, D), jnp.float32))
    (out_sum, grad_sum), grads = lax.scan(per_expert, start, jnp.arange(EXPERTS, dtype=jnp.int32))
    combined = out_sum[:TOKENS].astype(jnp.bfloat16)
    d_tokens = grad_sum[:TOKENS].astype(jnp.bfloat16)
    grad_gate_up = grads.reshape(N_EXPERT, D, 2, HALF)
    return combined, d_tokens, grad_gate_up
```

```python
import functools

import jax
import jax.numpy as jnp
from jax import lax
from jax.experimental import pallas as pl
from jax.experimental.pallas import tpu as pltpu
from jax.sharding import PartitionSpec as P

CAP = 8
NX = 8
NZ = 8
NY = 8
BF = jnp.bfloat16
F32 = jnp.float32
MESH = pl.DeviceIdType.MESH
ORDER = (4, 3, 5, 2, 6, 1, 7)


def iota(shape, dim):
    return lax.broadcasted_iota(jnp.int32, shape, dim)


def dot(a, b):
    return jnp.dot(a, b, preferred_element_type=F32)


def dot_nt(a, b):
    return lax.dot_general(a, b, (((1,), (1,)), ((), ())), preferred_element_type=F32)


def dot_tn(a, b):
    return lax.dot_general(a, b, (((0,), (0,)), ((), ())), preferred_element_type=F32)


def rank_table(meta, rows_of):
    n = meta.shape[0]
    mask = (meta > 0).astype(F32)
    i, j = iota((n, n), 0), iota((n, n), 1)
    lower = ((i // rows_of == j // rows_of) & (j < i)).astype(F32).astype(BF)
    rank = dot(lower, mask.astype(BF))
    return jnp.where(mask > 0, rank, -1.0).astype(BF)


def place_table(table, expert_of, blocks, rows_of):
    n = table.shape[0]
    per = blocks * CAP
    width = expert_of.shape[1]
    select = (iota((128, width), 0) == 64 + expert_of).astype(F32).astype(BF)
    rank = dot(table, select)
    col = iota((n, width), 1) % per
    row = iota((n, width), 0) // rows_of
    return ((rank == (col % CAP).astype(F32)) & (col // CAP == row)).astype(F32).astype(BF)


def kernel(
    tok, cot, routes, probs, wgu, wdn, comb_o, dtok_o, grad_o,
    s1z, s1x, c1x, a1z, a1x, b1z, b1x, g1, g2, q1, q2, d1, d2, perm, x2, xr, xt, cr, prow,
    pa, sb, rb, pb, pr, da, tb, ub, vb, vr, pre, hg, dg, y2, o1, o2, e1, e2, f1, f2, k1, k2,
    ss_a, rs_a, ss_d, rs_d, ss_c, rs_c, ss_p, rs_p, ss_g, rs_g, ss_w, rs_w, ss_e, rs_e, ss_k, rs_k,
):
    nx, nz, ny = NX, NZ, NY
    dp, ex = lax.axis_index("dp"), lax.axis_index("expert")
    y, c = dp // 2, dp % 2
    z, x = ex // nx, ex % nx
    rows_of, span = tok.shape
    tail = span - 256
    rows = nz * nx * CAP
    half = rows // 2
    piece = half // ny
    hid = wdn.shape[0]
    tile = min(128, half)
    nbx, nbz = [d for d in ORDER if d < nx], [d for d in ORDER if d < nz]
    nby = [d for d in ORDER if d < ny]

    def at(y_=None, c_=None, z_=None, x_=None):
        return (
            (y if y_ is None else y_) * 2 + (c if c_ is None else c_),
            (z if z_ is None else z_) * nx + (x if x_ is None else x_),
        )

    def remote(src, dst, ss, rs, dev):
        return pltpu.make_async_remote_copy(
            src_ref=src, dst_ref=dst, send_sem=ss, recv_sem=rs, device_id=dev, device_id_type=MESH
        )

    def send_x(src, dst, ss, rs):
        for d in nbx:
            p = (x + d) % nx
            remote(src(p), dst.at[x], ss.at[p], rs.at[x], at(x_=p)).start()

    def send_z(src, dst, ss, rs):
        for d in nbz:
            p = (z + d) % nz
            remote(src(p), dst.at[z], ss.at[p], rs.at[z], at(z_=p)).start()

    def send_y(src, dst, ss, rs):
        for d in nby:
            p = (y + d) % ny
            remote(src(p), dst, ss.at[p], rs.at[y], at(y_=p)).start()

    def got(dst, rs, me, others, n):
        for d in others[::-1]:
            p = (me + d) % n
            remote(dst(p), dst(p), rs.at[p], rs.at[p], at()).wait_recv()

    def sent(src, ss, me, others, n):
        for d in others:
            p = (me + d) % n
            remote(src(p), src(p), ss.at[p], ss.at[p], at()).wait_send()

    barrier = pltpu.get_barrier_semaphore()
    for d in nbx:
        pl.semaphore_signal(barrier, 1, device_id=at(x_=(x + d) % nx), device_id_type=MESH)
    for d in nbz:
        pl.semaphore_signal(barrier, 1, device_id=at(z_=(z + d) % nz), device_id_type=MESH)
    for d in nby:
        pl.semaphore_signal(barrier, 1, device_id=at(y_=(y + d) % ny), device_id_type=MESH)
    pl.semaphore_signal(barrier, 1, device_id=at(c_=1 - c), device_id_type=MESH)

    lane = iota((rows_of, 128), 1)
    weight = jnp.zeros((rows_of, 128), F32)
    for k in range(routes.shape[1]):
        weight += jnp.where(routes[:, k : k + 1] == lane % 32, probs[:, k : k + 1], 0.0)
    high = weight.astype(BF).astype(F32)
    meta = jnp.where(lane < 64, 0.0, jnp.where(lane < 96, high, weight - high))
    s1z[:, 0:256] = tok[:, 0:256]
    s1z[:, 256:384] = meta.astype(BF)
    s1x[...] = jnp.zeros_like(s1x)
    s1x[:, 0:tail] = tok[:, 256:span]
    s1x[:, 128:256] = (s1x[:, 128:256].astype(F32) + meta).astype(BF)
    c1x[...] = jnp.zeros_like(c1x)
    c1x[:, 0:tail] = cot[:, 256:span]
    pl.semaphore_wait(barrier, len(nbx) + len(nbz) + len(nby) + 1)

    send_z(lambda p: s1z, a1z, ss_a.at[0], rs_a.at[0])
    send_x(lambda p: s1x, a1x, ss_a.at[1], rs_a.at[1])
    send_z(lambda p: cot.at[:, 0:256], b1z, ss_a.at[2], rs_a.at[2])
    send_x(lambda p: c1x, b1x, ss_a.at[3], rs_a.at[3])
    a1z[z] = s1z[...]
    a1x[x] = s1x[...]
    b1z[z] = cot[:, 0:256]
    b1x[x] = c1x[...]
    r_, c_ = iota((rows, rows), 0), iota((rows, rows), 1)
    perm[...] = (
        (r_ // CAP // nz == c_ // CAP % nx) & (r_ // CAP % nz == c_ // CAP // nx) & (r_ % CAP == c_ % CAP)
    ).astype(F32).astype(BF)

    wide = (1, nx * nz * CAP)
    got(lambda p: a1z.at[p], rs_a.at[0], z, nbz, nz)
    block = a1z[...].reshape(nz * rows_of, 384)
    table = rank_table(block[:, 256:384].astype(F32), rows_of)
    g1[...] = place_table(table, z * (nx // 2) + iota(wide, 1) // (nz * CAP) // 2, nz, rows_of)
    q1[0] = dot_tn(g1[...], block[:, 0:256]).astype(BF).reshape(nx, nz * CAP, 256)
    send_x(lambda p: q1.at[0, p], d1.at[0], ss_d.at[0], rs_d.at[0])
    got(lambda p: a1x.at[p], rs_a.at[1], x, nbx, nx)
    block = a1x[...].reshape(nx * rows_of, 256)
    table = rank_table(block[:, 128:256].astype(F32) * (iota((nx * rows_of, 128), 1) >= 64), rows_of)
    g2[...] = place_table(table, iota(wide, 1) // (nx * CAP) * (nx // 2) + x // 2, nx, rows_of)
    q2[0] = dot_tn(g2[...], block).astype(BF).reshape(nz, nx * CAP, 256)
    send_z(lambda p: q2.at[0, p], d2.at[0], ss_d.at[1], rs_d.at[1])
    got(lambda p: b1z.at[p], rs_a.at[2], z, nbz, nz)
    q1[1] = dot_tn(g1[...], b1z[...].reshape(nz * rows_of, 256)).astype(BF).reshape(nx, nz * CAP, 256)
    send_x(lambda p: q1.at[1, p], d1.at[1], ss_d.at[2], rs_d.at[2])
    got(lambda p: b1x.at[p], rs_a.at[3], x, nbx, nx)
    q2[1] = dot_tn(g2[...], b1x[...].reshape(nx * rows_of, 256)).astype(BF).reshape(nz, nx * CAP, 256)
    send_z(lambda p: q2.at[1, p], d2.at[1], ss_d.at[3], rs_d.at[3])
    d1[0, x] = q1[0, x]
    d2[0, z] = q2[0, z]
    d1[1, x] = q1[1, x]
    d2[1, z] = q2[1, z]

    def sweep(n, body):
        def step(i, _):
            body(pl.ds(pl.multiple_of(i * tile, tile), tile), i * tile)
            return 0

        lax.fori_loop(0, n // tile, step, 0)

    got(lambda p: d1.at[0, p], rs_d.at[0], x, nbx, nx)
    got(lambda p: d2.at[0, p], rs_d.at[1], z, nbz, nz)
    expert = z * (nx // 2) + x // 2
    x2[...] = d2[0].reshape(rows, 256)

    def arrange(at_, _):
        lower = dot(perm[at_, :], x2[...])
        gate = lower[:, 128:256]
        which = iota((tile, 128), 1)
        gate = jnp.where((which == 64 + expert) | (which == 96 + expert), gate, 0.0)
        prow[at_, :] = jnp.broadcast_to(jnp.sum(gate, axis=1, keepdims=True), (tile, 128))
        xr[at_, 256:span] = lower[:, 0:tail].astype(BF)

    xr[:, 0:256] = d1[0].reshape(rows, 256)
    sweep(rows, arrange)
    mine, other = c * half, (1 - c) * half

    def pre_other(at_, i):
        src = pl.ds(pl.multiple_of(other + i, tile), tile)
        sb[at_, :] = dot(xr[src, :], wgu[...]).astype(BF)

    def pre_mine(at_, i):
        src = pl.ds(pl.multiple_of(mine + i, tile), tile)
        pa[at_, :] = dot(xr[src, :], wgu[...])

    sweep(half, pre_other)
    remote(sb, rb, ss_c.at[0], rs_c.at[0], at(c_=1 - c)).start()
    sweep(half, pre_mine)
    remote(sb, rb, ss_c.at[0], rs_c.at[0], at(c_=1 - c)).wait_recv()
    for d in nby:
        p = (y + d) % ny
        part = pl.ds(pl.multiple_of(p * piece, piece), piece)
        pb[p] = (pa[part, :] + rb[part, :].astype(F32)).astype(BF)
        remote(pb.at[p], pr.at[y], ss_p.at[0, p], rs_p.at[0, y], at(y_=p)).start()

    got(lambda p: d1.at[1, p], rs_d.at[2], x, nbx, nx)
    got(lambda p: d2.at[1, p], rs_d.at[3], z, nbz, nz)
    x2[...] = d2[1].reshape(rows, 256)

    def scale(at_, _):
        lower = dot(perm[at_, :], x2[...])
        gain = prow[at_, 0:1]
        cr[at_, 256:span] = (lower[:, 0:tail] * gain).astype(BF)
        cr[at_, 0:256] = (cr[at_, 0:256].astype(F32) * gain).astype(BF)

    cr[:, 0:256] = d1[1].reshape(rows, 256)
    sweep(rows, scale)

    def dh_other(at_, i):
        src = pl.ds(pl.multiple_of(other + i, tile), tile)
        tb[at_, :] = dot_nt(cr[src, :], wdn[...]).astype(BF)

    def dh_mine(at_, i):
        src = pl.ds(pl.multiple_of(mine + i, tile), tile)
        da[at_, :] = dot_nt(cr[src, :], wdn[...])

    sweep(half, dh_other)
    remote(tb, ub, ss_c.at[1], rs_c.at[1], at(c_=1 - c)).start()
    sweep(half, dh_mine)
    remote(tb, ub, ss_c.at[1], rs_c.at[1], at(c_=1 - c)).wait_recv()
    for d in nby:
        p = (y + d) % ny
        part = pl.ds(pl.multiple_of(p * piece, piece), piece)
        vb[p] = (da[part, :] + ub[part, :].astype(F32)).astype(BF)
        remote(vb.at[p], vr.at[y], ss_p.at[1, p], rs_p.at[1, y], at(y_=p)).start()

    here = pl.ds(pl.multiple_of(y * piece, piece), piece)
    pre[...] = pa[here, :] + rb[here, :].astype(F32)
    got(lambda p: pr.at[p], rs_p.at[0], y, nby, ny)
    for d in nby:
        pre[...] += pr[(y + d) % ny].astype(F32)
    gate, up = pre[:, 0:hid], pre[:, hid : 2 * hid]
    sig = 1.0 / (1.0 + jnp.exp(-gate))
    hg[c, y] = (gate * sig * up).astype(BF)
    send_y(lambda p: hg.at[c, y], hg.at[c, y], ss_g.at[0], rs_g.at[0])
    remote(hg.at[c, y], hg.at[c, y], ss_w.at[0, y], rs_w.at[0, y], at(c_=1 - c)).start()

    dh = da[here, :] + ub[here, :].astype(F32)
    got(lambda p: vr.at[p], rs_p.at[1], y, nby, ny)
    for d in nby:
        dh += vr[(y + d) % ny].astype(F32)
    gate, up = pre[:, 0:hid], pre[:, hid : 2 * hid]
    sig = 1.0 / (1.0 + jnp.exp(-gate))
    dg[c, y, :, 0:hid] = (dh * up * sig * (1.0 + gate * (1.0 - sig))).astype(BF)
    dg[c, y, :, hid : 2 * hid] = (dh * gate * sig).astype(BF)
    send_y(lambda p: dg.at[c, y], dg.at[c, y], ss_g.at[1], rs_g.at[1])
    remote(dg.at[c, y], dg.at[c, y], ss_w.at[1, y], rs_w.at[1, y], at(c_=1 - c)).start()

    y2[:, 128:256] = jnp.zeros((rows, 128), BF)
    xt[...] = dot_nt(
        (iota((span, span), 0) == iota((span, span), 1)).astype(F32).astype(BF), xr[...]
    ).astype(BF)

    def gather(buf, i):
        for d in nby[::-1]:
            p = (y + d) % ny
            remote(buf.at[c, p], buf.at[c, p], ss_g.at[i, p], rs_g.at[i, p], at()).wait_recv()
            remote(buf.at[c, p], buf.at[c, p], ss_w.at[i, p], rs_w.at[i, p], at(c_=1 - c)).start()
        for d in [0] + nby[::-1]:
            p = (y + d) % ny
            remote(buf.at[1 - c, p], buf.at[1 - c, p], ss_w.at[i, p], rs_w.at[i, p], at()).wait_recv()

    def back(i):
        o2[i] = dot(perm[...], y2[...]).astype(BF).reshape(nz, nx * CAP, 256)
        send_z(lambda p: o2.at[i, p], e2.at[i], ss_e.at[i, 1], rs_e.at[i, 1])
        e1[i, x] = o1[i, x]
        e2[i, z] = o2[i, z]

    def merge(i):
        got(lambda p: e1.at[i, p], rs_e.at[i, 0], x, nbx, nx)
        f1[i] = dot(g1[...], e1[i].reshape(nx * nz * CAP, 256)).astype(BF).reshape(nz, rows_of, 256)
        send_z(lambda p: f1.at[i, p], k1.at[i], ss_k.at[i, 0], rs_k.at[i, 0])
        got(lambda p: e2.at[i, p], rs_e.at[i, 1], z, nbz, nz)
        f2[i] = dot(g2[...], e2[i].reshape(nx * nz * CAP, 256)).astype(BF).reshape(nx, rows_of, 256)
        send_x(lambda p: f2.at[i, p], k2.at[i], ss_k.at[i, 1], rs_k.at[i, 1])
        k1[i, z] = f1[i, z]
        k2[i, x] = f2[i, x]

    def finish(i, out):
        got(lambda p: k1.at[i, p], rs_k.at[i, 0], z, nbz, nz)
        got(lambda p: k2.at[i, p], rs_k.at[i, 1], x, nbx, nx)
        out[:, 0:256] = jnp.sum(k1[i].astype(F32), axis=0).astype(BF)
        out[:, 256:span] = jnp.sum(k2[i].astype(F32), axis=0)[:, 0:tail].astype(BF)

    gather(hg, 0)
    per = nz * CAP

    def out_y(j, _):
        at_ = pl.ds(pl.multiple_of(j * per, per), per)
        own = hg[j // (nx // 2), pl.ds(j % (nx // 2) * (ny * 2 // nx), ny * 2 // nx)].reshape(per, hid)
        value = dot(own, wdn[...]) * prow[at_, 0:1]
        o1[0, j] = value[:, 0:256].astype(BF)
        y2[at_, 0:tail] = value[:, 256:span].astype(BF)
        return 0

    lax.fori_loop(0, nx, out_y, 0)
    send_x(lambda p: o1.at[0, p], e1.at[0], ss_e.at[0, 0], rs_e.at[0, 0])
    back(0)

    gather(dg, 1)

    def out_dx(j, _):
        at_ = pl.ds(pl.multiple_of(j * per, per), per)
        own = dg[j // (nx // 2), pl.ds(j % (nx // 2) * (ny * 2 // nx), ny * 2 // nx)].reshape(per, 2 * hid)
        value = dot_nt(own, wgu[...])
        o1[1, j] = value[:, 0:256].astype(BF)
        y2[at_, 0:tail] = value[:, 256:span].astype(BF)
        return 0

    lax.fori_loop(0, nx, out_dx, 0)
    send_x(lambda p: o1.at[1, p], e1.at[1], ss_e.at[1, 0], rs_e.at[1, 0])
    back(1)
    merge(0)

    step = span // 4

    def weights(j, _):
        at_ = pl.ds(pl.multiple_of(j * step, step), step)
        grad_o[at_, :] = dot(xt[at_, :], dg[...].reshape(rows, 2 * hid)).astype(BF)
        return 0

    lax.fori_loop(0, 4, weights, 0)
    merge(1)
    finish(0, comb_o)

    sent(lambda p: s1z, ss_a.at[0], z, nbz, nz)
    sent(lambda p: s1x, ss_a.at[1], x, nbx, nx)
    sent(lambda p: cot.at[:, 0:256], ss_a.at[2], z, nbz, nz)
    sent(lambda p: c1x, ss_a.at[3], x, nbx, nx)
    for i in range(2):
        sent(lambda p: q1.at[i, p], ss_d.at[2 * i], x, nbx, nx)
        sent(lambda p: q2.at[i, p], ss_d.at[2 * i + 1], z, nbz, nz)
        sent(lambda p: o1.at[i, p], ss_e.at[i, 0], x, nbx, nx)
        sent(lambda p: o2.at[i, p], ss_e.at[i, 1], z, nbz, nz)
    for i, (flat, parts, ring) in enumerate(((sb, pb, hg), (tb, vb, dg))):
        remote(flat, flat, ss_c.at[i], ss_c.at[i], at()).wait_send()
        sent(lambda p: parts.at[p], ss_p.at[i], y, nby, ny)
        sent(lambda p: ring.at[c, y], ss_g.at[i], y, nby, ny)
        sent(lambda p: ring.at[c, p], ss_w.at[i], y, [0] + nby, ny)
    finish(1, dtok_o)
    for i in range(2):
        sent(lambda p: f1.at[i, p], ss_k.at[i, 0], z, nbz, nz)
        sent(lambda p: f2.at[i, p], ss_k.at[i, 1], x, nbx, nx)


def shards(tokens, routes, probs, cotangent, w_gate_up, w_down):
    rows_of, span = tokens.shape
    hid = w_down.shape[1]
    nx, nz, ny = NX, NZ, NY
    rows = nx * nz * CAP
    half = rows // 2
    piece = half // ny
    vm, dma = pltpu.VMEM, pltpu.SemaphoreType.DMA
    n = max(nx, nz, ny)
    scratch = [
        vm((rows_of, 384), BF), vm((rows_of, 256), BF), vm((rows_of, 256), BF),
        vm((nz, rows_of, 384), BF), vm((nx, rows_of, 256), BF),
        vm((nz, rows_of, 256), BF), vm((nx, rows_of, 256), BF),
        vm((nz * rows_of, rows), BF), vm((nx * rows_of, rows), BF),
        vm((2, nx, nz * CAP, 256), BF), vm((2, nz, nx * CAP, 256), BF),
        vm((2, nx, nz * CAP, 256), BF), vm((2, nz, nx * CAP, 256), BF),
        vm((rows, rows), BF), vm((rows, 256), BF), vm((rows, span), BF), vm((span, rows), BF),
        vm((rows, span), BF), vm((rows, 128), F32),
        vm((half, 2 * hid), F32), vm((half, 2 * hid), BF), vm((half, 2 * hid), BF),
        vm((ny, piece, 2 * hid), BF), vm((ny, piece, 2 * hid), BF),
        vm((half, hid), F32), vm((half, hid), BF), vm((half, hid), BF),
        vm((ny, piece, hid), BF), vm((ny, piece, hid), BF),
        vm((piece, 2 * hid), F32),
        vm((2, ny, piece, hid), BF), vm((2, ny, piece, 2 * hid), BF),
        vm((rows, 256), BF),
        vm((2, nx, nz * CAP, 256), BF), vm((2, nz, nx * CAP, 256), BF),
        vm((2, nx, nz * CAP, 256), BF), vm((2, nz, nx * CAP, 256), BF),
        vm((2, nz, rows_of, 256), BF), vm((2, nx, rows_of, 256), BF),
        vm((2, nz, rows_of, 256), BF), vm((2, nx, rows_of, 256), BF),
        dma((4, n)), dma((4, n)), dma((4, n)), dma((4, n)), dma((2,)), dma((2,)),
        dma((2, n)), dma((2, n)), dma((2, n)), dma((2, n)), dma((2, n)), dma((2, n)),
        dma((2, 2, n)), dma((2, 2, n)), dma((2, 2, n)), dma((2, 2, n)),
    ]
    combined, d_tokens, grad = pl.pallas_call(
        kernel,
        out_shape=(
            jax.ShapeDtypeStruct((rows_of, span), BF),
            jax.ShapeDtypeStruct((rows_of, span), BF),
            jax.ShapeDtypeStruct((span, 2 * hid), BF),
        ),
        in_specs=[pl.BlockSpec(memory_space=pltpu.VMEM)] * 6,
        out_specs=[pl.BlockSpec(memory_space=pltpu.VMEM)] * 3,
        scratch_shapes=scratch,
        compiler_params=pltpu.CompilerParams(
            collective_id=0, has_side_effects=True, vmem_limit_bytes=48 * 2**20
        ),
        name="expert_layer",
    )(tokens, cotangent, routes, probs, w_gate_up.reshape(span, 2 * hid), w_down[0])
    return combined, d_tokens, grad.reshape(1, span, 2, hid)


def solution(mesh):
    placed = (
        P("expert", "dp"),
        P("expert", None),
        P("expert", None),
        P("expert", "dp"),
        P("expert", "dp", None, None),
        P("expert", None, "dp"),
    )
    return jax.shard_map(
        shards,
        mesh=mesh,
        in_specs=placed,
        out_specs=(P("expert", "dp"), P("expert", "dp"), P("expert", "dp", None, None)),
        check_vma=False,
    )
```

```python
import functools

import jax
import jax.numpy as jnp
from jax import lax
from jax.experimental import pallas as pl
from jax.experimental.pallas import tpu as pltpu
from jax.sharding import PartitionSpec as P

CAP = 8
PARTS = 2
SUB = CAP // PARTS
NX = 8
NZ = 8
NY = 8
BF = jnp.bfloat16
F32 = jnp.float32
MESH = pl.DeviceIdType.MESH
ORDER = (4, 3, 5, 2, 6, 1, 7)


def iota(shape, dim):
    return lax.broadcasted_iota(jnp.int32, shape, dim)


def dot(a, b):
    return jnp.dot(a, b, preferred_element_type=F32)


def dot_nt(a, b):
    return lax.dot_general(a, b, (((1,), (1,)), ((), ())), preferred_element_type=F32)


def dot_tn(a, b):
    return lax.dot_general(a, b, (((0,), (0,)), ((), ())), preferred_element_type=F32)


def rank_table(meta, rows_of):
    n = meta.shape[0]
    mask = (meta > 0).astype(F32)
    i, j = iota((n, n), 0), iota((n, n), 1)
    lower = ((i // rows_of == j // rows_of) & (j < i)).astype(F32).astype(BF)
    rank = dot(lower, mask.astype(BF))
    return jnp.where(mask > 0, rank, -1.0).astype(BF)


def place_table(table, expert_of, blocks, rows_of):
    n = table.shape[0]
    width = expert_of.shape[1]
    select = (iota((128, width), 0) == 64 + expert_of).astype(F32).astype(BF)
    rank = dot(table, select)
    col = iota((n, width), 1)
    row = iota((n, width), 0) // rows_of
    slot = col // (width // PARTS) * SUB + col % SUB
    return ((rank == slot.astype(F32)) & (col // SUB % blocks == row)).astype(F32).astype(BF)


def kernel(
    tok, cot, routes, probs, wgu, wdn, comb_o, dtok_o, grad_o,
    s1z, s1x, c1x, a1z, a1x, b1z, b1x, g1, g2, q1, q2, d1, d2, perm, x2, xr, xt, cr, prow,
    pa, sb, rb, pb, pq, pr, da, tb, ub, vb, vq, vr, pre, hg, dg, y2, o1, o2, e1, e2, f1, f2, k1, k2,
    ss_a, rs_a, ss_d, rs_d, ss_c, rs_c, ss_q, rs_q, ss_p, rs_p, ss_g, rs_g, ss_w, rs_w, ss_e, rs_e, ss_k, rs_k,
):
    nx, nz, ny = NX, NZ, NY
    dp, ex = lax.axis_index("dp"), lax.axis_index("expert")
    y, c = dp // 2, dp % 2
    z, x = ex // nx, ex % nx
    rows_of, span = tok.shape
    tail = span - 256
    rows = nz * nx * SUB
    half = rows // 2
    piece = half // ny
    hid = wdn.shape[1]
    tile = min(128, half)
    nbx, nbz = [d for d in ORDER if d < nx], [d for d in ORDER if d < nz]

    def at(y_=None, c_=None, z_=None, x_=None):
        return (
            (y if y_ is None else y_) * 2 + (c if c_ is None else c_),
            (z if z_ is None else z_) * nx + (x if x_ is None else x_),
        )

    def remote(src, dst, ss, rs, dev):
        return pltpu.make_async_remote_copy(
            src_ref=src, dst_ref=dst, send_sem=ss, recv_sem=rs, device_id=dev, device_id_type=MESH
        )

    def send_x(src, dst, ss, rs):
        for d in nbx:
            p = (x + d) % nx
            remote(src(p), dst.at[x], ss.at[p], rs.at[x], at(x_=p)).start()

    def send_z(src, dst, ss, rs):
        for d in nbz:
            p = (z + d) % nz
            remote(src(p), dst.at[z], ss.at[p], rs.at[z], at(z_=p)).start()

    def lanes(ref, cut):
        w = ref.shape[-1]
        return (pl.ds(0, w), pl.ds(0, w // 2), pl.ds(w // 2, w // 2))[cut]

    relays = ((2, 4, 1), (-2, -4, 2), (1, 3, 0), (-1, -3, 0))

    def near(d):
        return (y + d) % ny

    def reduce_first(i, value, out, land):
        for j, (d, far, cut) in enumerate(relays):
            out[j] = value(near(far)).astype(BF)
            at_ = lanes(out, cut)
            remote(out.at[j, :, at_], land.at[j, :, at_], ss_q.at[i, j], rs_q.at[i, j], at(y_=near(d))).start()

    def reduce_next(i, value, out, final):
        for j, d in ((0, 1), (1, -1)):
            out[4 + j] = value(near(d)).astype(BF)
            remote(out.at[4 + j], final.at[j], ss_p.at[i, j], rs_p.at[i, j], at(y_=near(d))).start()

    def reduce_relay(i, value, out, land, final):
        for j, d in ((2, 2), (3, -2)):
            part, whole = j - 2, j
            cut = lanes(land, j - 1)
            for ref, k in ((land.at[part, :, cut], part), (land.at[whole], whole)):
                remote(ref, ref, rs_q.at[i, k], rs_q.at[i, k], at()).wait_recv()
            total = value(near(d)) + land[whole].astype(F32)
            w = total.shape[1] // 2
            left, right = total[:, :w], total[:, w:]
            more = land[part, :, cut].astype(F32)
            out[4 + j, :, 0:w] = (left + more if j == 2 else left).astype(BF)
            out[4 + j, :, w : 2 * w] = (right if j == 2 else right + more).astype(BF)
            remote(out.at[4 + j], final.at[j], ss_p.at[i, j], rs_p.at[i, j], at(y_=near(d))).start()

    def reduce_done(i, total, final):
        for j in range(4):
            remote(final.at[j], final.at[j], rs_p.at[i, j], rs_p.at[i, j], at()).wait_recv()
            total += final[j].astype(F32)
        return total

    def reduce_sent(i, out):
        for j, (_, _, cut) in enumerate(relays):
            ref = out.at[j, :, lanes(out, cut)]
            remote(ref, ref, ss_q.at[i, j], ss_q.at[i, j], at()).wait_send()
            remote(out.at[4 + j], out.at[4 + j], ss_p.at[i, j], ss_p.at[i, j], at()).wait_send()

    hops = ((0, 2, 0), (0, -2, 0), (0, 1, 0), (0, -1, 0), (-2, 2, 1), (2, -2, 2), (-2, 1, 0), (2, -1, 0))
    origins = ((-2, 0), (2, 0), (-1, 0), (1, 0), (-4, 1), (4, 2), (-3, 0), (3, 0))

    def gather_send(i, buf, which):
        for k in which:
            origin, d, cut = hops[k]
            ref = buf.at[c, near(origin), :, lanes(buf, cut)]
            remote(ref, ref, ss_g.at[i, k], rs_g.at[i, k], at(y_=near(d))).start()

    def gather_got(i, buf, k):
        origin, cut = origins[k]
        ref = buf.at[c, near(origin), :, lanes(buf, cut)]
        remote(ref, ref, rs_g.at[i, k], rs_g.at[i, k], at()).wait_recv()

    def pass_on(i, buf, d):
        ref = buf.at[c, near(d)]
        remote(ref, ref, ss_w.at[i, near(d)], rs_w.at[i, near(d)], at(c_=1 - c)).start()

    def gather_first(i, buf):
        gather_send(i, buf, (0, 1, 2, 3))
        pass_on(i, buf, 0)

    def gather_relay(i, buf):
        gather_got(i, buf, 0)
        gather_send(i, buf, (4, 6))
        gather_got(i, buf, 1)
        gather_send(i, buf, (5, 7))
        pass_on(i, buf, -2)
        pass_on(i, buf, 2)
        for k, d in ((2, -1), (3, 1)):
            gather_got(i, buf, k)
            pass_on(i, buf, d)

    def gather_done(i, buf):
        for k, d in ((6, -3), (7, 3)):
            gather_got(i, buf, k)
            pass_on(i, buf, d)
        gather_got(i, buf, 4)
        gather_got(i, buf, 5)
        pass_on(i, buf, 4)
        for d in (0, -2, 2, -1, 1, -3, 3, 4):
            ref = buf.at[1 - c, near(d)]
            remote(ref, ref, rs_w.at[i, near(d)], rs_w.at[i, near(d)], at()).wait_recv()

    def gather_sent(i, buf):
        for k, (origin, _, cut) in enumerate(hops):
            ref = buf.at[c, near(origin), :, lanes(buf, cut)]
            remote(ref, ref, ss_g.at[i, k], ss_g.at[i, k], at()).wait_send()
        for d in range(ny):
            ref = buf.at[c, near(d)]
            remote(ref, ref, ss_w.at[i, near(d)], ss_w.at[i, near(d)], at()).wait_send()

    def got(dst, rs, me, others, n):
        for d in others[::-1]:
            p = (me + d) % n
            remote(dst(p), dst(p), rs.at[p], rs.at[p], at()).wait_recv()

    def sent(src, ss, me, others, n):
        for d in others:
            p = (me + d) % n
            remote(src(p), src(p), ss.at[p], ss.at[p], at()).wait_send()

    barrier = pltpu.get_barrier_semaphore()
    for d in nbx:
        pl.semaphore_signal(barrier, 1, device_id=at(x_=(x + d) % nx), device_id_type=MESH)
    for d in nbz:
        pl.semaphore_signal(barrier, 1, device_id=at(z_=(z + d) % nz), device_id_type=MESH)
    for d in (1, -1, 2, -2):
        pl.semaphore_signal(barrier, 1, device_id=at(y_=(y + d) % ny), device_id_type=MESH)
    pl.semaphore_signal(barrier, 1, device_id=at(c_=1 - c), device_id_type=MESH)

    weight = jnp.zeros((32, rows_of), F32)
    for k in range(routes.shape[0]):
        weight += jnp.where(routes[k : k + 1, :] == iota((32, rows_of), 0), probs[k : k + 1, :], 0.0)
    high = weight.astype(BF)
    low = (weight - high.astype(F32)).astype(BF)
    lane = iota((32, 128), 1) - iota((32, 128), 0)
    meta = dot_tn(high, (lane == 64).astype(F32).astype(BF)) + dot_tn(low, (lane == 96).astype(F32).astype(BF))
    s1z[:, 0:256] = tok[:, 0:256]
    s1z[:, 256:384] = meta.astype(BF)
    s1x[...] = jnp.zeros_like(s1x)
    s1x[:, 0:tail] = tok[:, 256:span]
    s1x[:, 128:256] = (s1x[:, 128:256].astype(F32) + meta).astype(BF)
    c1x[...] = jnp.zeros_like(c1x)
    c1x[:, 0:tail] = cot[:, 256:span]
    pl.semaphore_wait(barrier, len(nbx) + len(nbz) + 5)

    send_z(lambda p: s1z, a1z, ss_a.at[0], rs_a.at[0])
    send_x(lambda p: s1x, a1x, ss_a.at[1], rs_a.at[1])
    send_z(lambda p: cot.at[:, 0:256], b1z, ss_a.at[2], rs_a.at[2])
    send_x(lambda p: c1x, b1x, ss_a.at[3], rs_a.at[3])
    a1z[z] = s1z[...]
    a1x[x] = s1x[...]
    b1z[z] = cot[:, 0:256]
    b1x[x] = c1x[...]
    r_, c_ = iota((rows, rows), 0), iota((rows, rows), 1)
    perm[...] = (
        (r_ // SUB // nz == c_ // SUB % nx) & (r_ // SUB % nz == c_ // SUB // nx) & (r_ % SUB == c_ % SUB)
    ).astype(F32).astype(BF)

    wide = (1, PARTS * rows)
    dest = iota(wide, 1) % rows

    def pack(g, block, q):
        q[...] = dot_tn(g[...], block).astype(BF).reshape(q.shape)

    def slots_x(i, h):
        send_x(lambda p: q1.at[i, h, p], d1.at[i, h], ss_d.at[0, i, h], rs_d.at[0, i, h])
        d1[i, h, x] = q1[i, h, x]

    def slots_z(i, h):
        send_z(lambda p: q2.at[i, h, p], d2.at[i, h], ss_d.at[1, i, h], rs_d.at[1, i, h])
        d2[i, h, z] = q2[i, h, z]

    got(lambda p: a1z.at[p], rs_a.at[0], z, nbz, nz)
    block = a1z[...].reshape(nz * rows_of, 384)
    table = rank_table(block[:, 256:384].astype(F32), rows_of)
    g1[...] = place_table(table, z * (nx // 2) + dest // (nz * SUB) // 2, nz, rows_of)
    pack(g1, block[:, 0:256], q1.at[0])
    slots_x(0, 0)
    got(lambda p: a1x.at[p], rs_a.at[1], x, nbx, nx)
    block = a1x[...].reshape(nx * rows_of, 256)
    table = rank_table(block[:, 128:256].astype(F32) * (iota((nx * rows_of, 128), 1) >= 64), rows_of)
    g2[...] = place_table(table, dest // (nx * SUB) * (nx // 2) + x // 2, nx, rows_of)
    pack(g2, block, q2.at[0])
    slots_z(0, 0)
    slots_x(0, 1)
    slots_z(0, 1)
    got(lambda p: b1z.at[p], rs_a.at[2], z, nbz, nz)
    pack(g1, b1z[...].reshape(nz * rows_of, 256), q1.at[1])
    got(lambda p: b1x.at[p], rs_a.at[3], x, nbx, nx)
    pack(g2, b1x[...].reshape(nx * rows_of, 256), q2.at[1])
    for h in range(PARTS):
        slots_x(1, h)
        slots_z(1, h)

    def sweep(n, body):
        def step(i, _):
            body(pl.ds(pl.multiple_of(i * tile, tile), tile), i * tile)
            return 0

        lax.fori_loop(0, n // tile, step, 0)

    expert = z * (nx // 2) + x // 2
    mine, other = c * half, (1 - c) * half
    y2[:, :, 128:256] = jnp.zeros((PARTS, rows, 128), BF)

    def slots_got(i, h):
        got(lambda p: d1.at[i, h, p], rs_d.at[0, i, h], x, nbx, nx)
        got(lambda p: d2.at[i, h, p], rs_d.at[1, i, h], z, nbz, nz)

    def parts_of(src, weights, near_, far_, back_, i):
        def far_rows(at_, k):
            far_[at_, :] = dot(src[pl.ds(pl.multiple_of(other + k, tile), tile), :], weights[...]).astype(BF)

        def near_rows(at_, k):
            near_[at_, :] = dot(src[pl.ds(pl.multiple_of(mine + k, tile), tile), :], weights[...])

        sweep(half, far_rows)
        remote(far_, back_, ss_c.at[i], rs_c.at[i], at(c_=1 - c)).start()
        sweep(half, near_rows)

    def tokens_in(h):
        slots_got(0, h)
        x2[...] = d2[0, h].reshape(rows, 256)
        xr[h, :, 0:256] = d1[0, h].reshape(rows, 256)

        def arrange(at_, _):
            lower = dot(perm[at_, :], x2[...])
            gate = lower[:, 128:256]
            which = iota((tile, 128), 1)
            gate = jnp.where((which == 64 + expert) | (which == 96 + expert), gate, 0.0)
            prow[h, at_, :] = jnp.broadcast_to(jnp.sum(gate, axis=1, keepdims=True), (tile, 128))
            xr[h, at_, 256:span] = lower[:, 0:tail].astype(BF)

        sweep(rows, arrange)
        parts_of(xr.at[h], wgu, pa.at[h], sb.at[h], rb.at[h], h)

    def grads_in(h):
        slots_got(1, h)
        x2[...] = d2[1, h].reshape(rows, 256)
        cr[:, 0:256] = d1[1, h].reshape(rows, 256)

        def scale(at_, _):
            lower = dot(perm[at_, :], x2[...])
            gain = prow[h, at_, 0:1]
            cr[at_, 256:span] = (lower[:, 0:tail] * gain).astype(BF)
            cr[at_, 0:256] = (cr[at_, 0:256].astype(F32) * gain).astype(BF)

        sweep(rows, scale)
        parts_of(cr, wdn, da.at[h], tb.at[h], ub.at[h], 2 + h)

    def pre_sum(h):
        def value(p):
            part = pl.ds(pl.multiple_of(p * piece, piece), piece)
            return pa[h, part, :] + rb[h, part, :].astype(F32)

        return value

    def dh_sum(h):
        def value(p):
            part = pl.ds(pl.multiple_of(p * piece, piece), piece)
            return da[h, part, :] + ub[h, part, :].astype(F32)

        return value

    def pre_first(h):
        remote(rb.at[h], rb.at[h], rs_c.at[h], rs_c.at[h], at()).wait_recv()
        reduce_first(h, pre_sum(h), pb.at[h], pq.at[h])
        reduce_next(h, pre_sum(h), pb.at[h], pr.at[h])

    def dh_first(h):
        remote(ub.at[h], ub.at[h], rs_c.at[2 + h], rs_c.at[2 + h], at()).wait_recv()
        reduce_first(2 + h, dh_sum(h), vb.at[h], vq.at[h])
        reduce_next(2 + h, dh_sum(h), vb.at[h], vr.at[h])

    def pre_relay(h):
        reduce_relay(h, pre_sum(h), pb.at[h], pq.at[h], pr.at[h])

    def dh_relay(h):
        reduce_relay(2 + h, dh_sum(h), vb.at[h], vq.at[h], vr.at[h])

    def pre_done(h):
        pre[h] = reduce_done(h, pre_sum(h)(y), pr.at[h])
        gate, up = pre[h, :, 0:hid], pre[h, :, hid : 2 * hid]
        sig = 1.0 / (1.0 + jnp.exp(-gate))
        hg[h, c, y] = (gate * sig * up).astype(BF)
        gather_first(h, hg.at[h])

    def dh_done(h):
        dh = reduce_done(2 + h, dh_sum(h)(y), vr.at[h])
        gate, up = pre[h, :, 0:hid], pre[h, :, hid : 2 * hid]
        sig = 1.0 / (1.0 + jnp.exp(-gate))
        dg[h, c, y, :, 0:hid] = (dh * up * sig * (1.0 + gate * (1.0 - sig))).astype(BF)
        dg[h, c, y, :, hid : 2 * hid] = (dh * gate * sig).astype(BF)
        gather_first(2 + h, dg.at[h])

    def back(i, h, product, buf):
        full = buf[h].reshape(rows, buf.shape[-1])
        ways = tile // (nz * SUB)
        for j in range(rows // tile):
            value = product(full[j * tile : (j + 1) * tile], pl.ds(j * tile, tile))
            o1[i, h, j * ways : (j + 1) * ways] = value[:, 0:256].astype(BF).reshape(ways, nz * SUB, 256)
            y2[h, j * tile : (j + 1) * tile, 0:tail] = value[:, 256:span].astype(BF)
        send_x(lambda p: o1.at[i, h, p], e1.at[i, h], ss_e.at[0, i, h], rs_e.at[0, i, h])
        o2[i, h] = dot(perm[...], y2[h]).astype(BF).reshape(nz, nx * SUB, 256)
        send_z(lambda p: o2.at[i, h, p], e2.at[i, h], ss_e.at[1, i, h], rs_e.at[1, i, h])
        e1[i, h, x] = o1[i, h, x]
        e2[i, h, z] = o2[i, h, z]

    def back_y(h):
        back(0, h, lambda own, at_: dot_nt(own, wdn[...]) * prow[h, at_, 0:1], hg)

    def back_dx(h):
        back(1, h, lambda own, at_: dot_nt(own, wgu[...]), dg)

    def merge(i):
        for h in range(PARTS):
            got(lambda p: e1.at[i, h, p], rs_e.at[0, i, h], x, nbx, nx)
        f1[i] = dot(g1[...], e1[i].reshape(PARTS * rows, 256)).astype(BF).reshape(nz, rows_of, 256)
        send_z(lambda p: f1.at[i, p], k1.at[i], ss_k.at[i, 0], rs_k.at[i, 0])
        for h in range(PARTS):
            got(lambda p: e2.at[i, h, p], rs_e.at[1, i, h], z, nbz, nz)
        f2[i] = dot(g2[...], e2[i].reshape(PARTS * rows, 256)).astype(BF).reshape(nx, rows_of, 256)
        send_x(lambda p: f2.at[i, p], k2.at[i], ss_k.at[i, 1], rs_k.at[i, 1])
        k1[i, z] = f1[i, z]
        k2[i, x] = f2[i, x]

    def finish(i, out):
        got(lambda p: k1.at[i, p], rs_k.at[i, 0], z, nbz, nz)
        got(lambda p: k2.at[i, p], rs_k.at[i, 1], x, nbx, nx)
        out[:, 0:256] = jnp.sum(k1[i].astype(F32), axis=0).astype(BF)
        out[:, 256:span] = jnp.sum(k2[i].astype(F32), axis=0)[:, 0:tail].astype(BF)

    tokens_in(0)
    tokens_in(1)
    pre_first(0)
    grads_in(0)
    pre_first(1)
    dh_first(0)
    grads_in(1)
    pre_relay(0)
    dh_first(1)
    pre_relay(1)
    dh_relay(0)
    pre_done(0)
    dh_relay(1)
    pre_done(1)
    dh_done(0)
    gather_relay(0, hg.at[0])
    dh_done(1)
    gather_relay(1, hg.at[1])
    gather_relay(2, dg.at[0])
    gather_done(0, hg.at[0])
    back_y(0)
    gather_relay(3, dg.at[1])
    gather_done(1, hg.at[1])
    back_y(1)
    gather_done(2, dg.at[0])
    back_dx(0)
    gather_done(3, dg.at[1])
    back_dx(1)

    eye = (iota((span, span), 0) == iota((span, span), 1)).astype(F32).astype(BF)
    xt[...] = dot_nt(eye, xr[...].reshape(PARTS * rows, span)).astype(BF)
    step = span // 4

    def weights(j, _):
        at_ = pl.ds(pl.multiple_of(j * step, step), step)
        value = dot(xt[at_, :], dg[...].reshape(PARTS * rows, 2 * hid))
        for k in range(2):
            part = value[:, k * hid : (k + 1) * hid]
            grad_o[pl.ds(j * (step // 8), step // 8), k] = part.reshape(step // 8, 8, hid).astype(BF)
        return 0

    lax.fori_loop(0, 4, weights, 0)
    merge(0)
    merge(1)
    finish(0, comb_o)

    sent(lambda p: s1z, ss_a.at[0], z, nbz, nz)
    sent(lambda p: s1x, ss_a.at[1], x, nbx, nx)
    sent(lambda p: cot.at[:, 0:256], ss_a.at[2], z, nbz, nz)
    sent(lambda p: c1x, ss_a.at[3], x, nbx, nx)
    for h in range(PARTS):
        for i in range(2):
            sent(lambda p: q1.at[i, h, p], ss_d.at[0, i, h], x, nbx, nx)
            sent(lambda p: q2.at[i, h, p], ss_d.at[1, i, h], z, nbz, nz)
            sent(lambda p: o1.at[i, h, p], ss_e.at[0, i, h], x, nbx, nx)
            sent(lambda p: o2.at[i, h, p], ss_e.at[1, i, h], z, nbz, nz)
        for i, (flat, parts, ring) in enumerate(((sb, pb, hg), (tb, vb, dg))):
            j = 2 * i + h
            remote(flat.at[h], flat.at[h], ss_c.at[j], ss_c.at[j], at()).wait_send()
            reduce_sent(j, parts.at[h])
            gather_sent(j, ring.at[h])
    finish(1, dtok_o)
    for i in range(2):
        sent(lambda p: f1.at[i, p], ss_k.at[i, 0], z, nbz, nz)
        sent(lambda p: f2.at[i, p], ss_k.at[i, 1], x, nbx, nx)


def shards(tokens, routes, probs, cotangent, w_gate_up, w_down):
    rows_of, span = tokens.shape
    hid = w_down.shape[1]
    nx, nz, ny = NX, NZ, NY
    rows = nx * nz * SUB
    half = rows // 2
    piece = half // ny
    vm, dma = pltpu.VMEM, pltpu.SemaphoreType.DMA
    n = max(nx, nz, ny)
    h = PARTS
    along_x, along_z = vm((2, h, nx, nz * SUB, 256), BF), vm((2, h, nz, nx * SUB, 256), BF)
    scratch = [
        vm((rows_of, 384), BF), vm((rows_of, 256), BF), vm((rows_of, 256), BF),
        vm((nz, rows_of, 384), BF), vm((nx, rows_of, 256), BF),
        vm((nz, rows_of, 256), BF), vm((nx, rows_of, 256), BF),
        vm((nz * rows_of, h * rows), BF), vm((nx * rows_of, h * rows), BF),
        along_x, along_z, along_x, along_z,
        vm((rows, rows), BF), vm((rows, 256), BF), vm((h, rows, span), BF), vm((span, h * rows), BF),
        vm((rows, span), BF), vm((h, rows, 128), F32),
        vm((h, half, 2 * hid), F32), vm((h, half, 2 * hid), BF), vm((h, half, 2 * hid), BF),
        vm((h, 8, piece, 2 * hid), BF), vm((h, 4, piece, 2 * hid), BF), vm((h, 4, piece, 2 * hid), BF),
        vm((h, half, hid), F32), vm((h, half, hid), BF), vm((h, half, hid), BF),
        vm((h, 8, piece, hid), BF), vm((h, 4, piece, hid), BF), vm((h, 4, piece, hid), BF),
        vm((h, piece, 2 * hid), F32),
        vm((h, 2, ny, piece, hid), BF), vm((h, 2, ny, piece, 2 * hid), BF),
        vm((h, rows, 256), BF),
        along_x, along_z, along_x, along_z,
        vm((2, nz, rows_of, 256), BF), vm((2, nx, rows_of, 256), BF),
        vm((2, nz, rows_of, 256), BF), vm((2, nx, rows_of, 256), BF),
        dma((4, n)), dma((4, n)), dma((2, 2, h, n)), dma((2, 2, h, n)), dma((2 * h,)), dma((2 * h,)),
        dma((2 * h, 4)), dma((2 * h, 4)), dma((2 * h, 4)), dma((2 * h, 4)),
        dma((2 * h, 8)), dma((2 * h, 8)), dma((2 * h, n)), dma((2 * h, n)),
        dma((2, 2, h, n)), dma((2, 2, h, n)), dma((2, 2, n)), dma((2, 2, n)),
    ]
    combined, d_tokens, grad = pl.pallas_call(
        kernel,
        out_shape=(
            jax.ShapeDtypeStruct((rows_of, span), BF),
            jax.ShapeDtypeStruct((rows_of, span), BF),
            jax.ShapeDtypeStruct((span // 8, 2, 8, hid), BF),
        ),
        in_specs=[pl.BlockSpec(memory_space=pltpu.VMEM)] * 6,
        out_specs=[pl.BlockSpec(memory_space=pltpu.VMEM)] * 3,
        scratch_shapes=scratch,
        compiler_params=pltpu.CompilerParams(
            collective_id=0, has_side_effects=True, vmem_limit_bytes=48 * 2**20
        ),
        name="expert_layer",
    )(tokens, cotangent, routes.T, probs.T, w_gate_up.reshape(span, 2 * hid), w_down[0].T)
    return combined, d_tokens, grad.transpose(0, 2, 1, 3).reshape(1, span, 2, hid)


def solution(mesh):
    placed = (
        P("expert", "dp"),
        P("expert", None),
        P("expert", None),
        P("expert", "dp"),
        P("expert", "dp", None, None),
        P("expert", None, "dp"),
    )
    return jax.shard_map(
        shards,
        mesh=mesh,
        in_specs=placed,
        out_specs=(P("expert", "dp"), P("expert", "dp"), P("expert", "dp", None, None)),
        check_vma=False,
    )
```

```python
import functools

import jax
import jax.numpy as jnp
from jax import lax
from jax.experimental import pallas as pl
from jax.experimental.pallas import tpu as pltpu
from jax.sharding import PartitionSpec as P

CAP = 8
PARTS = 2
SUB = CAP // PARTS
NX = 8
NZ = 8
NY = 8
BF = jnp.bfloat16
F32 = jnp.float32
MESH = pl.DeviceIdType.MESH
ORDER = (4, 3, 5, 2, 6, 1, 7)
DIRECT = ()
SPREAD = ()


def iota(shape, dim):
    return lax.broadcasted_iota(jnp.int32, shape, dim)


def dot(a, b):
    return jnp.dot(a, b, preferred_element_type=F32)


def dot_nt(a, b):
    return lax.dot_general(a, b, (((1,), (1,)), ((), ())), preferred_element_type=F32)


def dot_tn(a, b):
    return lax.dot_general(a, b, (((0,), (0,)), ((), ())), preferred_element_type=F32)


def rank_table(meta, lower):
    mask = (meta > 0).astype(F32)
    return jnp.where(mask > 0, dot(lower, mask.astype(BF)), -1.0).astype(BF)


def place_plan(expert_of, blocks, rows_of, select, want):
    n, width = want.shape
    select[...] = (iota((128, width), 0) == 64 + expert_of).astype(F32).astype(BF)
    col = iota((1, width), 1)
    slot = (col // (width // PARTS) * SUB + col % SUB).astype(F32)
    want[...] = jnp.where(col // SUB % blocks == iota((n, width), 0) // rows_of, slot, -2.0)


def kernel(
    tok, cot, routes, probs, wgu3, wdn, comb_o, dtok_o, grad_o,
    s1z, s1x, c1x, a1z, a1x, b1z, b1x, g1, g2, q1, q2, d1, d2, wgu, perm, tri, sel1, sel2, want1, want2, x2, xr, xt, cr, prow,
    pa, sb, rb, pb, pq, pr, da, tb, ub, vb, vq, vr, pre, hg, dg, y2, o1, o2, e1, e2, f1, f2, k1, k2,
    ss_a, rs_a, ss_d, rs_d, ss_c, rs_c, ss_q, rs_q, ss_p, rs_p, ss_g, rs_g, ss_w, rs_w, ss_e, rs_e, ss_k, rs_k,
):
    nx, nz, ny = NX, NZ, NY
    dp, ex = lax.axis_index("dp"), lax.axis_index("expert")
    y, c = dp // 2, dp % 2
    z, x = ex // nx, ex % nx
    rows_of, span = tok.shape
    tail = span - 256
    rows = nz * nx * SUB
    half = rows // 2
    piece = half // ny
    hid = wdn.shape[1]
    tile = min(128, half)
    nbx, nbz = [d for d in ORDER if d < nx], [d for d in ORDER if d < nz]

    def at(y_=None, c_=None, z_=None, x_=None):
        return (
            (y if y_ is None else y_) * 2 + (c if c_ is None else c_),
            (z if z_ is None else z_) * nx + (x if x_ is None else x_),
        )

    def remote(src, dst, ss, rs, dev):
        return pltpu.make_async_remote_copy(
            src_ref=src, dst_ref=dst, send_sem=ss, recv_sem=rs, device_id=dev, device_id_type=MESH
        )

    def send_x(src, dst, ss, rs):
        for d in nbx:
            p = (x + d) % nx
            remote(src(p), dst.at[x], ss.at[p], rs.at[x], at(x_=p)).start()

    def send_z(src, dst, ss, rs):
        for d in nbz:
            p = (z + d) % nz
            remote(src(p), dst.at[z], ss.at[p], rs.at[z], at(z_=p)).start()

    def lanes(ref, cut):
        w = ref.shape[-1]
        return (pl.ds(0, w), pl.ds(0, w // 2), pl.ds(w // 2, w // 2))[cut]

    relays = ((2, 4, 1), (-2, -4, 2), (1, 3, 0), (-1, -3, 0))

    turn = (4, 3, -3, 2, -2, 1, -1)

    def near(d):
        return (y + d) % ny

    def reduce_first(i, value, out, land, final):
        if i in DIRECT:
            for d in turn:
                p = near(d)
                out[p] = value(p).astype(BF)
                remote(out.at[p], final.at[y], ss_p.at[i, p], rs_p.at[i, y], at(y_=p)).start()
            return
        for j, (d, far, cut) in enumerate(relays):
            out[j] = value(near(far)).astype(BF)
            at_ = lanes(out, cut)
            remote(out.at[j, :, at_], land.at[j, :, at_], ss_q.at[i, j], rs_q.at[i, j], at(y_=near(d))).start()

    def reduce_next(i, value, out, final):
        if i in DIRECT:
            return
        for j, d in ((0, 1), (1, -1)):
            out[4 + j] = value(near(d)).astype(BF)
            remote(out.at[4 + j], final.at[j], ss_p.at[i, j], rs_p.at[i, j], at(y_=near(d))).start()

    def reduce_relay(i, value, out, land, final):
        if i in DIRECT:
            return
        for j, d in ((2, 2), (3, -2)):
            part, whole = j - 2, j
            cut = lanes(land, j - 1)
            for ref, k in ((land.at[part, :, cut], part), (land.at[whole], whole)):
                remote(ref, ref, rs_q.at[i, k], rs_q.at[i, k], at()).wait_recv()
            total = value(near(d)) + land[whole].astype(F32)
            w = total.shape[1] // 2
            left, right = total[:, :w], total[:, w:]
            more = land[part, :, cut].astype(F32)
            out[4 + j, :, 0:w] = (left + more if j == 2 else left).astype(BF)
            out[4 + j, :, w : 2 * w] = (right if j == 2 else right + more).astype(BF)
            remote(out.at[4 + j], final.at[j], ss_p.at[i, j], rs_p.at[i, j], at(y_=near(d))).start()

    def reduce_done(i, total, final):
        for j in [near(d) for d in turn[::-1]] if i in DIRECT else range(4):
            remote(final.at[j], final.at[j], rs_p.at[i, j], rs_p.at[i, j], at()).wait_recv()
            total += final[j].astype(F32)
        return total

    def reduce_sent(i, out):
        if i in DIRECT:
            for d in turn:
                p = near(d)
                remote(out.at[p], out.at[p], ss_p.at[i, p], ss_p.at[i, p], at()).wait_send()
            return
        for j, (_, _, cut) in enumerate(relays):
            ref = out.at[j, :, lanes(out, cut)]
            remote(ref, ref, ss_q.at[i, j], ss_q.at[i, j], at()).wait_send()
            remote(out.at[4 + j], out.at[4 + j], ss_p.at[i, j], ss_p.at[i, j], at()).wait_send()

    hops = ((0, 2, 0), (0, -2, 0), (0, 1, 0), (0, -1, 0), (-2, 2, 1), (2, -2, 2), (-2, 1, 0), (2, -1, 0))
    origins = ((-2, 0), (2, 0), (-1, 0), (1, 0), (-4, 1), (4, 2), (-3, 0), (3, 0))

    def gather_send(i, buf, which):
        for k in which:
            origin, d, cut = hops[k]
            ref = buf.at[c, near(origin), :, lanes(buf, cut)]
            remote(ref, ref, ss_g.at[i, k], rs_g.at[i, k], at(y_=near(d))).start()

    def gather_got(i, buf, k):
        origin, cut = origins[k]
        ref = buf.at[c, near(origin), :, lanes(buf, cut)]
        remote(ref, ref, rs_g.at[i, k], rs_g.at[i, k], at()).wait_recv()

    def pass_on(i, buf, d):
        ref = buf.at[c, near(d)]
        remote(ref, ref, ss_w.at[i, near(d)], rs_w.at[i, near(d)], at(c_=1 - c)).start()

    def gather_first(i, buf):
        if i in SPREAD:
            for d in turn:
                p = near(d)
                remote(buf.at[c, y], buf.at[c, y], ss_g.at[i, p], rs_g.at[i, y], at(y_=p)).start()
        else:
            gather_send(i, buf, (0, 1, 2, 3))
        pass_on(i, buf, 0)

    def gather_relay(i, buf):
        if i in SPREAD:
            return
        gather_got(i, buf, 0)
        gather_send(i, buf, (4, 6))
        gather_got(i, buf, 1)
        gather_send(i, buf, (5, 7))
        pass_on(i, buf, -2)
        pass_on(i, buf, 2)
        for k, d in ((2, -1), (3, 1)):
            gather_got(i, buf, k)
            pass_on(i, buf, d)

    def gather_done(i, buf):
        if i in SPREAD:
            for d in turn[::-1]:
                ref = buf.at[c, near(d)]
                remote(ref, ref, rs_g.at[i, near(d)], rs_g.at[i, near(d)], at()).wait_recv()
                pass_on(i, buf, d)
        else:
            for k, d in ((6, -3), (7, 3)):
                gather_got(i, buf, k)
                pass_on(i, buf, d)
            gather_got(i, buf, 4)
            gather_got(i, buf, 5)
            pass_on(i, buf, 4)
        for d in (0, -2, 2, -1, 1, -3, 3, 4):
            ref = buf.at[1 - c, near(d)]
            remote(ref, ref, rs_w.at[i, near(d)], rs_w.at[i, near(d)], at()).wait_recv()

    def gather_sent(i, buf):
        if i in SPREAD:
            for d in turn:
                remote(buf.at[c, y], buf.at[c, y], ss_g.at[i, near(d)], ss_g.at[i, near(d)], at()).wait_send()
        else:
            for k, (origin, _, cut) in enumerate(hops):
                ref = buf.at[c, near(origin), :, lanes(buf, cut)]
                remote(ref, ref, ss_g.at[i, k], ss_g.at[i, k], at()).wait_send()
        for d in range(ny):
            ref = buf.at[c, near(d)]
            remote(ref, ref, ss_w.at[i, near(d)], ss_w.at[i, near(d)], at()).wait_send()

    def got(dst, rs, me, others, n):
        for d in others[::-1]:
            p = (me + d) % n
            remote(dst(p), dst(p), rs.at[p], rs.at[p], at()).wait_recv()

    def sent(src, ss, me, others, n):
        for d in others:
            p = (me + d) % n
            remote(src(p), src(p), ss.at[p], ss.at[p], at()).wait_send()

    barrier = pltpu.get_barrier_semaphore()
    for d in nbx:
        pl.semaphore_signal(barrier, 1, device_id=at(x_=(x + d) % nx), device_id_type=MESH)
    for d in nbz:
        pl.semaphore_signal(barrier, 1, device_id=at(z_=(z + d) % nz), device_id_type=MESH)
    for d in (1, -1, 2, -2):
        pl.semaphore_signal(barrier, 1, device_id=at(y_=(y + d) % ny), device_id_type=MESH)
    pl.semaphore_signal(barrier, 1, device_id=at(c_=1 - c), device_id_type=MESH)

    weight = jnp.zeros((32, rows_of), F32)
    for k in range(routes.shape[0]):
        weight += jnp.where(routes[k : k + 1, :] == iota((32, rows_of), 0), probs[k : k + 1, :], 0.0)
    high = weight.astype(BF)
    low = (weight - high.astype(F32)).astype(BF)
    lane = iota((32, 128), 1) - iota((32, 128), 0)
    meta = dot_tn(high, (lane == 64).astype(F32).astype(BF)) + dot_tn(low, (lane == 96).astype(F32).astype(BF))
    s1z[:, 0:256] = tok[:, 0:256]
    s1z[:, 256:384] = meta.astype(BF)
    s1x[...] = jnp.zeros_like(s1x)
    s1x[:, 0:tail] = tok[:, 256:span]
    s1x[:, 128:256] = (s1x[:, 128:256].astype(F32) + meta).astype(BF)
    c1x[...] = jnp.zeros_like(c1x)
    c1x[:, 0:tail] = cot[:, 256:span]
    pl.semaphore_wait(barrier, len(nbx) + len(nbz) + 5)

    send_z(lambda p: s1z, a1z, ss_a.at[0], rs_a.at[0])
    send_x(lambda p: s1x, a1x, ss_a.at[1], rs_a.at[1])
    send_z(lambda p: cot.at[:, 0:256], b1z, ss_a.at[2], rs_a.at[2])
    send_x(lambda p: c1x, b1x, ss_a.at[3], rs_a.at[3])
    a1z[z] = s1z[...]
    a1x[x] = s1x[...]
    b1z[z] = cot[:, 0:256]
    b1x[x] = c1x[...]
    r_, c_ = iota((rows, rows), 0), iota((rows, rows), 1)
    perm[...] = (
        (r_ // SUB // nz == c_ // SUB % nx) & (r_ // SUB % nz == c_ // SUB // nx) & (r_ % SUB == c_ % SUB)
    ).astype(F32).astype(BF)

    wgu[...] = wgu3[...].reshape(span, 2 * hid)
    wide = (1, PARTS * rows)
    dest = iota(wide, 1) % rows
    r_, c_ = iota(tri.shape, 0), iota(tri.shape, 1)
    tri[...] = ((r_ // rows_of == c_ // rows_of) & (c_ < r_)).astype(F32).astype(BF)
    place_plan(z * (nx // 2) + dest // (nz * SUB) // 2, nz, rows_of, sel1, want1)
    place_plan(dest // (nx * SUB) * (nx // 2) + x // 2, nx, rows_of, sel2, want2)

    def placed(meta, sel, want):
        return (dot(rank_table(meta, tri[...]), sel[...]) == want[...]).astype(F32).astype(BF)


    def pack(g, block, q):
        q[...] = dot_tn(g[...], block).astype(BF).reshape(q.shape)

    def slots_x(i, h):
        send_x(lambda p: q1.at[i, h, p], d1.at[i, h], ss_d.at[0, i, h], rs_d.at[0, i, h])
        d1[i, h, x] = q1[i, h, x]

    def slots_z(i, h):
        send_z(lambda p: q2.at[i, h, p], d2.at[i, h], ss_d.at[1, i, h], rs_d.at[1, i, h])
        d2[i, h, z] = q2[i, h, z]

    got(lambda p: a1z.at[p], rs_a.at[0], z, nbz, nz)
    block = a1z[...].reshape(nz * rows_of, 384)
    g1[...] = placed(block[:, 256:384].astype(F32), sel1, want1)
    pack(g1, block[:, 0:256], q1.at[0])
    slots_x(0, 0)
    got(lambda p: a1x.at[p], rs_a.at[1], x, nbx, nx)
    block = a1x[...].reshape(nx * rows_of, 256)
    g2[...] = placed(jnp.where(iota((nx * rows_of, 128), 1) >= 64, block[:, 128:256].astype(F32), 0.0), sel2, want2)
    pack(g2, block, q2.at[0])
    slots_z(0, 0)
    slots_x(0, 1)
    slots_z(0, 1)
    got(lambda p: b1z.at[p], rs_a.at[2], z, nbz, nz)
    pack(g1, b1z[...].reshape(nz * rows_of, 256), q1.at[1])
    got(lambda p: b1x.at[p], rs_a.at[3], x, nbx, nx)
    pack(g2, b1x[...].reshape(nx * rows_of, 256), q2.at[1])
    for h in range(PARTS):
        slots_x(1, h)
        slots_z(1, h)

    expert = z * (nx // 2) + x // 2
    mine, other = c * half, (1 - c) * half
    y2[:, :, 128:256] = jnp.zeros((PARTS, rows, 128), BF)

    def slots_got(i, h):
        got(lambda p: d1.at[i, h, p], rs_d.at[0, i, h], x, nbx, nx)
        got(lambda p: d2.at[i, h, p], rs_d.at[1, i, h], z, nbz, nz)

    def parts_of(arrange, src, weights, near_, far_, back_, i):
        at_ = pl.ds(pl.multiple_of(other, half), half)
        arrange(at_)
        far_[...] = dot(src[at_, :], weights[...]).astype(BF)
        remote(far_, back_, ss_c.at[i], rs_c.at[i], at(c_=1 - c)).start()
        at_ = pl.ds(pl.multiple_of(mine, half), half)
        arrange(at_)
        near_[...] = dot(src[at_, :], weights[...])

    def tokens_in(h):
        slots_got(0, h)
        xr[h, :, 0:256] = d1[0, h].reshape(rows, 256)

        def arrange(at_):
            xr[h, at_, 256:span] = dot(perm[at_, :], d2[0, h].reshape(rows, 256))[:, 0:tail].astype(BF)

        parts_of(arrange, xr.at[h], wgu, pa.at[h], sb.at[h], rb.at[h], h)

    def gains(h):
        gate = dot(perm[...], d2[0, h].reshape(rows, 256)[:, 128:256])
        which = iota((rows, 128), 1)
        gate = jnp.where((which == 64 + expert) | (which == 96 + expert), gate, 0.0)
        prow[h] = jnp.broadcast_to(jnp.sum(gate, axis=1, keepdims=True), (rows, 128))

    def grads_in(h):
        slots_got(1, h)
        x2[...] = d1[1, h].reshape(rows, 256)

        def arrange(at_):
            gain = prow[h, at_, 0:1]
            cr[at_, 0:256] = (x2[at_, :].astype(F32) * gain).astype(BF)
            lower = dot(perm[at_, :], d2[1, h].reshape(rows, 256))
            cr[at_, 256:span] = (lower[:, 0:tail] * gain).astype(BF)

        parts_of(arrange, cr, wdn, da.at[h], tb.at[h], ub.at[h], 2 + h)

    def pre_sum(h):
        def value(p):
            part = pl.ds(pl.multiple_of(p * piece, piece), piece)
            return pa[h, part, :] + rb[h, part, :].astype(F32)

        return value

    def dh_sum(h):
        def value(p):
            part = pl.ds(pl.multiple_of(p * piece, piece), piece)
            return da[h, part, :] + ub[h, part, :].astype(F32)

        return value

    def pre_first(h):
        remote(rb.at[h], rb.at[h], rs_c.at[h], rs_c.at[h], at()).wait_recv()
        reduce_first(h, pre_sum(h), pb.at[h], pq.at[h], pr.at[h])
        reduce_next(h, pre_sum(h), pb.at[h], pr.at[h])

    def dh_first(h):
        remote(ub.at[h], ub.at[h], rs_c.at[2 + h], rs_c.at[2 + h], at()).wait_recv()
        reduce_first(2 + h, dh_sum(h), vb.at[h], vq.at[h], vr.at[h])
        reduce_next(2 + h, dh_sum(h), vb.at[h], vr.at[h])

    def pre_relay(h):
        reduce_relay(h, pre_sum(h), pb.at[h], pq.at[h], pr.at[h])

    def dh_relay(h):
        reduce_relay(2 + h, dh_sum(h), vb.at[h], vq.at[h], vr.at[h])

    def pre_done(h):
        pre[h] = reduce_done(h, pre_sum(h)(y), pr.at[h])
        gate, up = pre[h, :, 0:hid], pre[h, :, hid : 2 * hid]
        sig = 1.0 / (1.0 + jnp.exp(-gate))
        hg[h, c, y] = (gate * sig * up).astype(BF)
        gather_first(h, hg.at[h])

    def dh_done(h):
        dh = reduce_done(2 + h, dh_sum(h)(y), vr.at[h])
        gate, up = pre[h, :, 0:hid], pre[h, :, hid : 2 * hid]
        sig = 1.0 / (1.0 + jnp.exp(-gate))
        dg[h, c, y, :, 0:hid] = (dh * up * sig * (1.0 + gate * (1.0 - sig))).astype(BF)
        dg[h, c, y, :, hid : 2 * hid] = (dh * gate * sig).astype(BF)
        gather_first(2 + h, dg.at[h])

    def back(i, h, product, buf):
        full = buf[h].reshape(rows, buf.shape[-1])
        ways = tile // (nz * SUB)
        for j in range(rows // tile):
            value = product(full[j * tile : (j + 1) * tile], pl.ds(j * tile, tile))
            o1[i, h, j * ways : (j + 1) * ways] = value[:, 0:256].astype(BF).reshape(ways, nz * SUB, 256)
            y2[h, j * tile : (j + 1) * tile, 0:tail] = value[:, 256:span].astype(BF)
        send_x(lambda p: o1.at[i, h, p], e1.at[i, h], ss_e.at[0, i, h], rs_e.at[0, i, h])
        o2[i, h] = dot(perm[...], y2[h]).astype(BF).reshape(nz, nx * SUB, 256)
        send_z(lambda p: o2.at[i, h, p], e2.at[i, h], ss_e.at[1, i, h], rs_e.at[1, i, h])
        e1[i, h, x] = o1[i, h, x]
        e2[i, h, z] = o2[i, h, z]

    def back_y(h):
        back(0, h, lambda own, at_: dot_nt(own, wdn[...]) * prow[h, at_, 0:1], hg)

    def back_dx(h):
        back(1, h, lambda own, at_: dot_nt(own, wgu[...]), dg)

    def merge(i):
        for h in range(PARTS):
            got(lambda p: e1.at[i, h, p], rs_e.at[0, i, h], x, nbx, nx)
        f1[i] = dot(g1[...], e1[i].reshape(PARTS * rows, 256)).astype(BF).reshape(nz, rows_of, 256)
        send_z(lambda p: f1.at[i, p], k1.at[i], ss_k.at[i, 0], rs_k.at[i, 0])
        for h in range(PARTS):
            got(lambda p: e2.at[i, h, p], rs_e.at[1, i, h], z, nbz, nz)
        f2[i] = dot(g2[...], e2[i].reshape(PARTS * rows, 256)).astype(BF).reshape(nx, rows_of, 256)
        send_x(lambda p: f2.at[i, p], k2.at[i], ss_k.at[i, 1], rs_k.at[i, 1])
        k1[i, z] = f1[i, z]
        k2[i, x] = f2[i, x]

    def finish(i, out):
        got(lambda p: k1.at[i, p], rs_k.at[i, 0], z, nbz, nz)
        got(lambda p: k2.at[i, p], rs_k.at[i, 1], x, nbx, nx)
        out[:, 0:256] = jnp.sum(k1[i].astype(F32), axis=0).astype(BF)
        out[:, 256:span] = jnp.sum(k2[i].astype(F32), axis=0)[:, 0:tail].astype(BF)

    tokens_in(0)
    gains(0)
    tokens_in(1)
    gains(1)
    pre_first(0)
    grads_in(0)
    pre_first(1)
    dh_first(0)
    grads_in(1)
    pre_relay(0)
    dh_first(1)
    pre_relay(1)
    dh_relay(0)
    pre_done(0)
    dh_relay(1)
    pre_done(1)
    dh_done(0)
    gather_relay(0, hg.at[0])
    dh_done(1)
    gather_relay(1, hg.at[1])
    gather_relay(2, dg.at[0])
    gather_done(0, hg.at[0])
    back_y(0)
    gather_relay(3, dg.at[1])
    gather_done(1, hg.at[1])
    back_y(1)
    gather_done(2, dg.at[0])
    back_dx(0)
    gather_done(3, dg.at[1])
    back_dx(1)

    eye = (iota((span, span), 0) == iota((span, span), 1)).astype(F32).astype(BF)
    xt[...] = dot_nt(eye, xr[...].reshape(PARTS * rows, span)).astype(BF)
    step = span // 4

    def weights(j, _):
        at_ = pl.ds(pl.multiple_of(j * step, step), step)
        value = dot(xt[at_, :], dg[...].reshape(PARTS * rows, 2 * hid))
        grad_o[at_] = value.reshape(step, 2, hid).astype(BF)
        return 0

    lax.fori_loop(0, 4, weights, 0)
    merge(0)
    merge(1)
    finish(0, comb_o)

    sent(lambda p: s1z, ss_a.at[0], z, nbz, nz)
    sent(lambda p: s1x, ss_a.at[1], x, nbx, nx)
    sent(lambda p: cot.at[:, 0:256], ss_a.at[2], z, nbz, nz)
    sent(lambda p: c1x, ss_a.at[3], x, nbx, nx)
    for h in range(PARTS):
        for i in range(2):
            sent(lambda p: q1.at[i, h, p], ss_d.at[0, i, h], x, nbx, nx)
            sent(lambda p: q2.at[i, h, p], ss_d.at[1, i, h], z, nbz, nz)
            sent(lambda p: o1.at[i, h, p], ss_e.at[0, i, h], x, nbx, nx)
            sent(lambda p: o2.at[i, h, p], ss_e.at[1, i, h], z, nbz, nz)
        for i, (flat, parts, ring) in enumerate(((sb, pb, hg), (tb, vb, dg))):
            j = 2 * i + h
            remote(flat.at[h], flat.at[h], ss_c.at[j], ss_c.at[j], at()).wait_send()
            reduce_sent(j, parts.at[h])
            gather_sent(j, ring.at[h])
    finish(1, dtok_o)
    for i in range(2):
        sent(lambda p: f1.at[i, p], ss_k.at[i, 0], z, nbz, nz)
        sent(lambda p: f2.at[i, p], ss_k.at[i, 1], x, nbx, nx)


def shards(tokens, routes, probs, cotangent, w_gate_up, w_down):
    rows_of, span = tokens.shape
    hid = w_down.shape[1]
    nx, nz, ny = NX, NZ, NY
    rows = nx * nz * SUB
    half = rows // 2
    piece = half // ny
    vm, dma = pltpu.VMEM, pltpu.SemaphoreType.DMA
    n = max(nx, nz, ny)
    h = PARTS
    along_x, along_z = vm((2, h, nx, nz * SUB, 256), BF), vm((2, h, nz, nx * SUB, 256), BF)
    scratch = [
        vm((rows_of, 384), BF), vm((rows_of, 256), BF), vm((rows_of, 256), BF),
        vm((nz, rows_of, 384), BF), vm((nx, rows_of, 256), BF),
        vm((nz, rows_of, 256), BF), vm((nx, rows_of, 256), BF),
        vm((nz * rows_of, h * rows), BF), vm((nx * rows_of, h * rows), BF),
        along_x, along_z, along_x, along_z,
        vm((span, 2 * hid), BF), vm((rows, rows), BF), vm((nz * rows_of, nz * rows_of), BF),
        vm((128, h * rows), BF), vm((128, h * rows), BF),
        vm((nz * rows_of, h * rows), F32), vm((nx * rows_of, h * rows), F32),
        vm((rows, 256), BF), vm((h, rows, span), BF), vm((span, h * rows), BF),
        vm((rows, span), BF), vm((h, rows, 128), F32),
        vm((h, half, 2 * hid), F32), vm((h, half, 2 * hid), BF), vm((h, half, 2 * hid), BF),
        vm((h, 8, piece, 2 * hid), BF), vm((h, 4, piece, 2 * hid), BF), vm((h, 8, piece, 2 * hid), BF),
        vm((h, half, hid), F32), vm((h, half, hid), BF), vm((h, half, hid), BF),
        vm((h, 8, piece, hid), BF), vm((h, 4, piece, hid), BF), vm((h, 8, piece, hid), BF),
        vm((h, piece, 2 * hid), F32),
        vm((h, 2, ny, piece, hid), BF), vm((h, 2, ny, piece, 2 * hid), BF),
        vm((h, rows, 256), BF),
        along_x, along_z, along_x, along_z,
        vm((2, nz, rows_of, 256), BF), vm((2, nx, rows_of, 256), BF),
        vm((2, nz, rows_of, 256), BF), vm((2, nx, rows_of, 256), BF),
        dma((4, n)), dma((4, n)), dma((2, 2, h, n)), dma((2, 2, h, n)), dma((2 * h,)), dma((2 * h,)),
        dma((2 * h, 4)), dma((2 * h, 4)), dma((2 * h, 8)), dma((2 * h, 8)),
        dma((2 * h, 8)), dma((2 * h, 8)), dma((2 * h, n)), dma((2 * h, n)),
        dma((2, 2, h, n)), dma((2, 2, h, n)), dma((2, 2, n)), dma((2, 2, n)),
    ]
    combined, d_tokens, grad = pl.pallas_call(
        kernel,
        out_shape=(
            jax.ShapeDtypeStruct((rows_of, span), BF),
            jax.ShapeDtypeStruct((rows_of, span), BF),
            jax.ShapeDtypeStruct((span, 2, hid), BF),
        ),
        in_specs=[pl.BlockSpec(memory_space=pltpu.VMEM)] * 6,
        out_specs=[pl.BlockSpec(memory_space=pltpu.VMEM)] * 3,
        scratch_shapes=scratch,
        compiler_params=pltpu.CompilerParams(
            collective_id=0, has_side_effects=True, vmem_limit_bytes=48 * 2**20
        ),
        name="expert_layer",
    )(tokens, cotangent, routes.T, probs.T, w_gate_up[0], w_down[0].T)
    return combined, d_tokens, grad[None]


def solution(mesh):
    placed = (
        P("expert", "dp"),
        P("expert", None),
        P("expert", None),
        P("expert", "dp"),
        P("expert", "dp", None, None),
        P("expert", None, "dp"),
    )
    return jax.shard_map(
        shards,
        mesh=mesh,
        in_specs=placed,
        out_specs=(P("expert", "dp"), P("expert", "dp"), P("expert", "dp", None, None)),
        check_vma=False,
    )
```

```python
import functools

import jax
import jax.numpy as jnp
from jax import lax
from jax.experimental import pallas as pl
from jax.experimental.pallas import tpu as pltpu
from jax.sharding import PartitionSpec as P

CAP = 8
PARTS = 2
SUB = CAP // PARTS
NX = 8
NZ = 8
NY = 8
BF = jnp.bfloat16
F32 = jnp.float32
MESH = pl.DeviceIdType.MESH
ORDER = (4, 3, 5, 2, 6, 1, 7)


def iota(shape, dim):
    return lax.broadcasted_iota(jnp.int32, shape, dim)


def dot(a, b):
    return jnp.dot(a, b, preferred_element_type=F32)


def dot_nt(a, b):
    return lax.dot_general(a, b, (((1,), (1,)), ((), ())), preferred_element_type=F32)


def dot_tn(a, b):
    return lax.dot_general(a, b, (((0,), (0,)), ((), ())), preferred_element_type=F32)


def rank_table(meta, rows_of):
    n = meta.shape[0]
    mask = (meta > 0).astype(F32)
    i, j = iota((n, n), 0), iota((n, n), 1)
    lower = ((i // rows_of == j // rows_of) & (j < i)).astype(F32).astype(BF)
    rank = dot(lower, mask.astype(BF))
    return jnp.where(mask > 0, rank, -1.0).astype(BF)


def place_table(table, expert_of, blocks, rows_of):
    n = table.shape[0]
    width = expert_of.shape[1]
    select = (iota((128, width), 0) == 64 + expert_of).astype(F32).astype(BF)
    rank = dot(table, select)
    col = iota((n, width), 1)
    row = iota((n, width), 0) // rows_of
    slot = col // (width // PARTS) * SUB + col % SUB
    return ((rank == slot.astype(F32)) & (col // SUB % blocks == row)).astype(F32).astype(BF)


def kernel(
    tok, cot, routes, probs, wgu, wdn, comb_o, dtok_o, grad_o,
    s1z, s1x, c1x, a1z, a1x, b1z, b1x, g1, g2, q1, q2, d1, d2, perm, x2, xr, xt, cr, prow,
    pa, sb, rb, pb, pq, pr, da, tb, ub, vb, vq, vr, pre, hg, dg, y2, o1, o2, e1, e2, f1, f2, k1, k2,
    ss_a, rs_a, ss_d, rs_d, ss_c, rs_c, ss_q, rs_q, ss_p, rs_p, ss_g, rs_g, ss_w, rs_w, ss_e, rs_e, ss_k, rs_k,
):
    nx, nz, ny = NX, NZ, NY
    dp, ex = lax.axis_index("dp"), lax.axis_index("expert")
    y, c = dp // 2, dp % 2
    z, x = ex // nx, ex % nx
    rows_of, span = tok.shape
    tail = span - 256
    rows = nz * nx * SUB
    half = rows // 2
    piece = half // ny
    hid = wdn.shape[1]
    tile = min(128, half)
    nbx, nbz = [d for d in ORDER if d < nx], [d for d in ORDER if d < nz]

    def at(y_=None, c_=None, z_=None, x_=None):
        return (
            (y if y_ is None else y_) * 2 + (c if c_ is None else c_),
            (z if z_ is None else z_) * nx + (x if x_ is None else x_),
        )

    def remote(src, dst, ss, rs, dev):
        return pltpu.make_async_remote_copy(
            src_ref=src, dst_ref=dst, send_sem=ss, recv_sem=rs, device_id=dev, device_id_type=MESH
        )

    def send_x(src, dst, ss, rs):
        for d in nbx:
            p = (x + d) % nx
            remote(src(p), dst.at[x], ss.at[p], rs.at[x], at(x_=p)).start()

    def send_z(src, dst, ss, rs):
        for d in nbz:
            p = (z + d) % nz
            remote(src(p), dst.at[z], ss.at[p], rs.at[z], at(z_=p)).start()

    def lanes(ref, cut):
        w = ref.shape[-1]
        return (pl.ds(0, w), pl.ds(0, w // 2), pl.ds(w // 2, w // 2))[cut]

    relays = ((2, 4, 1), (-2, -4, 2), (1, 3, 0), (-1, -3, 0))

    def near(d):
        return (y + d) % ny

    def reduce_first(i, value, out, land):
        for j, (d, far, cut) in enumerate(relays):
            out[j] = value(near(far)).astype(BF)
            at_ = lanes(out, cut)
            remote(out.at[j, :, at_], land.at[j, :, at_], ss_q.at[i, j], rs_q.at[i, j], at(y_=near(d))).start()

    def reduce_next(i, value, out, final):
        for j, d in ((0, 1), (1, -1)):
            out[4 + j] = value(near(d)).astype(BF)
            remote(out.at[4 + j], final.at[j], ss_p.at[i, j], rs_p.at[i, j], at(y_=near(d))).start()

    def reduce_relay(i, value, out, land, final):
        for j, d in ((2, 2), (3, -2)):
            part, whole = j - 2, j
            cut = lanes(land, j - 1)
            for ref, k in ((land.at[part, :, cut], part), (land.at[whole], whole)):
                remote(ref, ref, rs_q.at[i, k], rs_q.at[i, k], at()).wait_recv()
            total = value(near(d)) + land[whole].astype(F32)
            w = total.shape[1] // 2
            left, right = total[:, :w], total[:, w:]
            more = land[part, :, cut].astype(F32)
            out[4 + j, :, 0:w] = (left + more if j == 2 else left).astype(BF)
            out[4 + j, :, w : 2 * w] = (right if j == 2 else right + more).astype(BF)
            remote(out.at[4 + j], final.at[j], ss_p.at[i, j], rs_p.at[i, j], at(y_=near(d))).start()

    def reduce_done(i, total, final):
        for j in range(4):
            remote(final.at[j], final.at[j], rs_p.at[i, j], rs_p.at[i, j], at()).wait_recv()
            total += final[j].astype(F32)
        return total

    def reduce_sent(i, out):
        for j, (_, _, cut) in enumerate(relays):
            ref = out.at[j, :, lanes(out, cut)]
            remote(ref, ref, ss_q.at[i, j], ss_q.at[i, j], at()).wait_send()
            remote(out.at[4 + j], out.at[4 + j], ss_p.at[i, j], ss_p.at[i, j], at()).wait_send()

    hops = ((0, 2, 0), (0, -2, 0), (0, 1, 0), (0, -1, 0), (-2, 2, 1), (2, -2, 2), (-2, 1, 0), (2, -1, 0))
    origins = ((-2, 0), (2, 0), (-1, 0), (1, 0), (-4, 1), (4, 2), (-3, 0), (3, 0))

    def gather_send(i, buf, which):
        for k in which:
            origin, d, cut = hops[k]
            ref = buf.at[c, near(origin), :, lanes(buf, cut)]
            remote(ref, ref, ss_g.at[i, k], rs_g.at[i, k], at(y_=near(d))).start()

    def gather_got(i, buf, k):
        origin, cut = origins[k]
        ref = buf.at[c, near(origin), :, lanes(buf, cut)]
        remote(ref, ref, rs_g.at[i, k], rs_g.at[i, k], at()).wait_recv()

    def pass_on(i, buf, d):
        ref = buf.at[c, near(d)]
        remote(ref, ref, ss_w.at[i, near(d)], rs_w.at[i, near(d)], at(c_=1 - c)).start()

    def gather_first(i, buf):
        gather_send(i, buf, (0, 1, 2, 3))
        pass_on(i, buf, 0)

    def gather_relay(i, buf):
        gather_got(i, buf, 0)
        gather_send(i, buf, (4, 6))
        gather_got(i, buf, 1)
        gather_send(i, buf, (5, 7))
        pass_on(i, buf, -2)
        pass_on(i, buf, 2)
        for k, d in ((2, -1), (3, 1)):
            gather_got(i, buf, k)
            pass_on(i, buf, d)

    def gather_done(i, buf):
        for k, d in ((6, -3), (7, 3)):
            gather_got(i, buf, k)
            pass_on(i, buf, d)
        gather_got(i, buf, 4)
        gather_got(i, buf, 5)
        pass_on(i, buf, 4)
        for d in (0, -2, 2, -1, 1, -3, 3, 4):
            ref = buf.at[1 - c, near(d)]
            remote(ref, ref, rs_w.at[i, near(d)], rs_w.at[i, near(d)], at()).wait_recv()

    def gather_sent(i, buf):
        for k, (origin, _, cut) in enumerate(hops):
            ref = buf.at[c, near(origin), :, lanes(buf, cut)]
            remote(ref, ref, ss_g.at[i, k], ss_g.at[i, k], at()).wait_send()
        for d in range(ny):
            ref = buf.at[c, near(d)]
            remote(ref, ref, ss_w.at[i, near(d)], ss_w.at[i, near(d)], at()).wait_send()

    def got(dst, rs, me, others, n):
        for d in others[::-1]:
            p = (me + d) % n
            remote(dst(p), dst(p), rs.at[p], rs.at[p], at()).wait_recv()

    def sent(src, ss, me, others, n):
        for d in others:
            p = (me + d) % n
            remote(src(p), src(p), ss.at[p], ss.at[p], at()).wait_send()

    barrier = pltpu.get_barrier_semaphore()
    for d in nbx:
        pl.semaphore_signal(barrier, 1, device_id=at(x_=(x + d) % nx), device_id_type=MESH)
    for d in nbz:
        pl.semaphore_signal(barrier, 1, device_id=at(z_=(z + d) % nz), device_id_type=MESH)
    for d in (1, -1, 2, -2):
        pl.semaphore_signal(barrier, 1, device_id=at(y_=(y + d) % ny), device_id_type=MESH)
    pl.semaphore_signal(barrier, 1, device_id=at(c_=1 - c), device_id_type=MESH)

    weight = jnp.zeros((32, rows_of), F32)
    for k in range(routes.shape[0]):
        weight += jnp.where(routes[k : k + 1, :] == iota((32, rows_of), 0), probs[k : k + 1, :], 0.0)
    high = weight.astype(BF)
    low = (weight - high.astype(F32)).astype(BF)
    lane = iota((32, 128), 1) - iota((32, 128), 0)
    meta = dot_tn(high, (lane == 64).astype(F32).astype(BF)) + dot_tn(low, (lane == 96).astype(F32).astype(BF))
    s1z[:, 0:256] = tok[:, 0:256]
    s1z[:, 256:384] = meta.astype(BF)
    s1x[...] = jnp.zeros_like(s1x)
    s1x[:, 0:tail] = tok[:, 256:span]
    s1x[:, 128:256] = (s1x[:, 128:256].astype(F32) + meta).astype(BF)
    c1x[...] = jnp.zeros_like(c1x)
    c1x[:, 0:tail] = cot[:, 256:span]
    pl.semaphore_wait(barrier, len(nbx) + len(nbz) + 5)

    send_z(lambda p: s1z, a1z, ss_a.at[0], rs_a.at[0])
    send_x(lambda p: s1x, a1x, ss_a.at[1], rs_a.at[1])
    send_z(lambda p: cot.at[:, 0:256], b1z, ss_a.at[2], rs_a.at[2])
    send_x(lambda p: c1x, b1x, ss_a.at[3], rs_a.at[3])
    a1z[z] = s1z[...]
    a1x[x] = s1x[...]
    b1z[z] = cot[:, 0:256]
    b1x[x] = c1x[...]
    r_, c_ = iota((rows, rows), 0), iota((rows, rows), 1)
    perm[...] = (
        (r_ // SUB // nz == c_ // SUB % nx) & (r_ // SUB % nz == c_ // SUB // nx) & (r_ % SUB == c_ % SUB)
    ).astype(F32).astype(BF)

    wide = (1, PARTS * rows)
    dest = iota(wide, 1) % rows

    def pack(g, block, q):
        q[...] = dot_tn(g[...], block).astype(BF).reshape(q.shape)

    def slots_x(i, h):
        send_x(lambda p: q1.at[i, h, p], d1.at[i, h], ss_d.at[0, i, h], rs_d.at[0, i, h])
        d1[i, h, x] = q1[i, h, x]

    def slots_z(i, h):
        send_z(lambda p: q2.at[i, h, p], d2.at[i, h], ss_d.at[1, i, h], rs_d.at[1, i, h])
        d2[i, h, z] = q2[i, h, z]

    got(lambda p: a1z.at[p], rs_a.at[0], z, nbz, nz)
    block = a1z[...].reshape(nz * rows_of, 384)
    table = rank_table(block[:, 256:384].astype(F32), rows_of)
    g1[...] = place_table(table, z * (nx // 2) + dest // (nz * SUB) // 2, nz, rows_of)
    pack(g1, block[:, 0:256], q1.at[0])
    slots_x(0, 0)
    got(lambda p: a1x.at[p], rs_a.at[1], x, nbx, nx)
    block = a1x[...].reshape(nx * rows_of, 256)
    table = rank_table(block[:, 128:256].astype(F32) * (iota((nx * rows_of, 128), 1) >= 64), rows_of)
    g2[...] = place_table(table, dest // (nx * SUB) * (nx // 2) + x // 2, nx, rows_of)
    pack(g2, block, q2.at[0])
    slots_z(0, 0)
    slots_x(0, 1)
    slots_z(0, 1)
    got(lambda p: b1z.at[p], rs_a.at[2], z, nbz, nz)
    pack(g1, b1z[...].reshape(nz * rows_of, 256), q1.at[1])
    got(lambda p: b1x.at[p], rs_a.at[3], x, nbx, nx)
    pack(g2, b1x[...].reshape(nx * rows_of, 256), q2.at[1])
    for h in range(PARTS):
        slots_x(1, h)
        slots_z(1, h)

    def sweep(n, body):
        def step(i, _):
            body(pl.ds(pl.multiple_of(i * tile, tile), tile), i * tile)
            return 0

        lax.fori_loop(0, n // tile, step, 0)

    expert = z * (nx // 2) + x // 2
    mine, other = c * half, (1 - c) * half
    y2[:, :, 128:256] = jnp.zeros((PARTS, rows, 128), BF)

    def slots_got(i, h):
        got(lambda p: d1.at[i, h, p], rs_d.at[0, i, h], x, nbx, nx)
        got(lambda p: d2.at[i, h, p], rs_d.at[1, i, h], z, nbz, nz)

    def parts_of(src, weights, near_, far_, back_, i):
        def far_rows(at_, k):
            far_[at_, :] = dot(src[pl.ds(pl.multiple_of(other + k, tile), tile), :], weights[...]).astype(BF)

        def near_rows(at_, k):
            near_[at_, :] = dot(src[pl.ds(pl.multiple_of(mine + k, tile), tile), :], weights[...])

        sweep(half, far_rows)
        remote(far_, back_, ss_c.at[i], rs_c.at[i], at(c_=1 - c)).start()
        sweep(half, near_rows)

    def tokens_in(h):
        slots_got(0, h)
        x2[...] = d2[0, h].reshape(rows, 256)
        xr[h, :, 0:256] = d1[0, h].reshape(rows, 256)

        def arrange(at_, _):
            lower = dot(perm[at_, :], x2[...])
            gate = lower[:, 128:256]
            which = iota((tile, 128), 1)
            gate = jnp.where((which == 64 + expert) | (which == 96 + expert), gate, 0.0)
            prow[h, at_, :] = jnp.broadcast_to(jnp.sum(gate, axis=1, keepdims=True), (tile, 128))
            xr[h, at_, 256:span] = lower[:, 0:tail].astype(BF)

        sweep(rows, arrange)
        parts_of(xr.at[h], wgu, pa.at[h], sb.at[h], rb.at[h], h)

    def grads_in(h):
        slots_got(1, h)
        x2[...] = d2[1, h].reshape(rows, 256)
        cr[:, 0:256] = d1[1, h].reshape(rows, 256)

        def scale(at_, _):
            lower = dot(perm[at_, :], x2[...])
            gain = prow[h, at_, 0:1]
            cr[at_, 256:span] = (lower[:, 0:tail] * gain).astype(BF)
            cr[at_, 0:256] = (cr[at_, 0:256].astype(F32) * gain).astype(BF)

        sweep(rows, scale)
        parts_of(cr, wdn, da.at[h], tb.at[h], ub.at[h], 2 + h)

    def pre_sum(h):
        def value(p):
            part = pl.ds(pl.multiple_of(p * piece, piece), piece)
            return pa[h, part, :] + rb[h, part, :].astype(F32)

        return value

    def dh_sum(h):
        def value(p):
            part = pl.ds(pl.multiple_of(p * piece, piece), piece)
            return da[h, part, :] + ub[h, part, :].astype(F32)

        return value

    def pre_first(h):
        remote(rb.at[h], rb.at[h], rs_c.at[h], rs_c.at[h], at()).wait_recv()
        reduce_first(h, pre_sum(h), pb.at[h], pq.at[h])
        reduce_next(h, pre_sum(h), pb.at[h], pr.at[h])

    def dh_first(h):
        remote(ub.at[h], ub.at[h], rs_c.at[2 + h], rs_c.at[2 + h], at()).wait_recv()
        reduce_first(2 + h, dh_sum(h), vb.at[h], vq.at[h])
        reduce_next(2 + h, dh_sum(h), vb.at[h], vr.at[h])

    def pre_relay(h):
        reduce_relay(h, pre_sum(h), pb.at[h], pq.at[h], pr.at[h])

    def dh_relay(h):
        reduce_relay(2 + h, dh_sum(h), vb.at[h], vq.at[h], vr.at[h])

    def pre_done(h):
        pre[h] = reduce_done(h, pre_sum(h)(y), pr.at[h])
        gate, up = pre[h, :, 0:hid], pre[h, :, hid : 2 * hid]
        sig = 1.0 / (1.0 + jnp.exp(-gate))
        hg[h, c, y] = (gate * sig * up).astype(BF)
        gather_first(h, hg.at[h])

    def dh_done(h):
        dh = reduce_done(2 + h, dh_sum(h)(y), vr.at[h])
        gate, up = pre[h, :, 0:hid], pre[h, :, hid : 2 * hid]
        sig = 1.0 / (1.0 + jnp.exp(-gate))
        dg[h, c, y, :, 0:hid] = (dh * up * sig * (1.0 + gate * (1.0 - sig))).astype(BF)
        dg[h, c, y, :, hid : 2 * hid] = (dh * gate * sig).astype(BF)
        gather_first(2 + h, dg.at[h])

    def back(i, h, product, buf):
        full = buf[h].reshape(rows, buf.shape[-1])
        ways = tile // (nz * SUB)
        for j in range(rows // tile):
            value = product(full[j * tile : (j + 1) * tile], pl.ds(j * tile, tile))
            o1[i, h, j * ways : (j + 1) * ways] = value[:, 0:256].astype(BF).reshape(ways, nz * SUB, 256)
            y2[h, j * tile : (j + 1) * tile, 0:tail] = value[:, 256:span].astype(BF)
        send_x(lambda p: o1.at[i, h, p], e1.at[i, h], ss_e.at[0, i, h], rs_e.at[0, i, h])
        o2[i, h] = dot(perm[...], y2[h]).astype(BF).reshape(nz, nx * SUB, 256)
        send_z(lambda p: o2.at[i, h, p], e2.at[i, h], ss_e.at[1, i, h], rs_e.at[1, i, h])
        e1[i, h, x] = o1[i, h, x]
        e2[i, h, z] = o2[i, h, z]

    def back_y(h):
        back(0, h, lambda own, at_: dot_nt(own, wdn[...]) * prow[h, at_, 0:1], hg)

    def back_dx(h):
        back(1, h, lambda own, at_: dot_nt(own, wgu[...]), dg)

    def merge(i):
        for h in range(PARTS):
            got(lambda p: e1.at[i, h, p], rs_e.at[0, i, h], x, nbx, nx)
        f1[i] = dot(g1[...], e1[i].reshape(PARTS * rows, 256)).astype(BF).reshape(nz, rows_of, 256)
        send_z(lambda p: f1.at[i, p], k1.at[i], ss_k.at[i, 0], rs_k.at[i, 0])
        for h in range(PARTS):
            got(lambda p: e2.at[i, h, p], rs_e.at[1, i, h], z, nbz, nz)
        f2[i] = dot(g2[...], e2[i].reshape(PARTS * rows, 256)).astype(BF).reshape(nx, rows_of, 256)
        send_x(lambda p: f2.at[i, p], k2.at[i], ss_k.at[i, 1], rs_k.at[i, 1])
        k1[i, z] = f1[i, z]
        k2[i, x] = f2[i, x]

    def finish(i, out):
        got(lambda p: k1.at[i, p], rs_k.at[i, 0], z, nbz, nz)
        got(lambda p: k2.at[i, p], rs_k.at[i, 1], x, nbx, nx)
        out[:, 0:256] = jnp.sum(k1[i].astype(F32), axis=0).astype(BF)
        out[:, 256:span] = jnp.sum(k2[i].astype(F32), axis=0)[:, 0:tail].astype(BF)

    tokens_in(0)
    tokens_in(1)
    pre_first(0)
    grads_in(0)
    pre_first(1)
    dh_first(0)
    grads_in(1)
    pre_relay(0)
    dh_first(1)
    pre_relay(1)
    dh_relay(0)
    pre_done(0)
    dh_relay(1)
    pre_done(1)
    dh_done(0)
    gather_relay(0, hg.at[0])
    dh_done(1)
    gather_relay(1, hg.at[1])
    gather_relay(2, dg.at[0])
    gather_done(0, hg.at[0])
    back_y(0)
    gather_relay(3, dg.at[1])
    gather_done(1, hg.at[1])
    back_y(1)
    gather_done(2, dg.at[0])
    back_dx(0)
    gather_done(3, dg.at[1])
    back_dx(1)

    eye = (iota((span, span), 0) == iota((span, span), 1)).astype(F32).astype(BF)
    xt[...] = dot_nt(eye, xr[...].reshape(PARTS * rows, span)).astype(BF)
    step = span // 4

    def weights(j, _):
        at_ = pl.ds(pl.multiple_of(j * step, step), step)
        value = dot(xt[at_, :], dg[...].reshape(PARTS * rows, 2 * hid))
        grad_o[at_] = value.reshape(step, 2, hid).astype(BF)
        return 0

    lax.fori_loop(0, 4, weights, 0)
    merge(0)
    merge(1)
    finish(0, comb_o)

    sent(lambda p: s1z, ss_a.at[0], z, nbz, nz)
    sent(lambda p: s1x, ss_a.at[1], x, nbx, nx)
    sent(lambda p: cot.at[:, 0:256], ss_a.at[2], z, nbz, nz)
    sent(lambda p: c1x, ss_a.at[3], x, nbx, nx)
    for h in range(PARTS):
        for i in range(2):
            sent(lambda p: q1.at[i, h, p], ss_d.at[0, i, h], x, nbx, nx)
            sent(lambda p: q2.at[i, h, p], ss_d.at[1, i, h], z, nbz, nz)
            sent(lambda p: o1.at[i, h, p], ss_e.at[0, i, h], x, nbx, nx)
            sent(lambda p: o2.at[i, h, p], ss_e.at[1, i, h], z, nbz, nz)
        for i, (flat, parts, ring) in enumerate(((sb, pb, hg), (tb, vb, dg))):
            j = 2 * i + h
            remote(flat.at[h], flat.at[h], ss_c.at[j], ss_c.at[j], at()).wait_send()
            reduce_sent(j, parts.at[h])
            gather_sent(j, ring.at[h])
    finish(1, dtok_o)
    for i in range(2):
        sent(lambda p: f1.at[i, p], ss_k.at[i, 0], z, nbz, nz)
        sent(lambda p: f2.at[i, p], ss_k.at[i, 1], x, nbx, nx)


def shards(tokens, routes, probs, cotangent, w_gate_up, w_down):
    rows_of, span = tokens.shape
    hid = w_down.shape[1]
    nx, nz, ny = NX, NZ, NY
    rows = nx * nz * SUB
    half = rows // 2
    piece = half // ny
    vm, dma = pltpu.VMEM, pltpu.SemaphoreType.DMA
    n = max(nx, nz, ny)
    h = PARTS
    along_x, along_z = vm((2, h, nx, nz * SUB, 256), BF), vm((2, h, nz, nx * SUB, 256), BF)
    scratch = [
        vm((rows_of, 384), BF), vm((rows_of, 256), BF), vm((rows_of, 256), BF),
        vm((nz, rows_of, 384), BF), vm((nx, rows_of, 256), BF),
        vm((nz, rows_of, 256), BF), vm((nx, rows_of, 256), BF),
        vm((nz * rows_of, h * rows), BF), vm((nx * rows_of, h * rows), BF),
        along_x, along_z, along_x, along_z,
        vm((rows, rows), BF), vm((rows, 256), BF), vm((h, rows, span), BF), vm((span, h * rows), BF),
        vm((rows, span), BF), vm((h, rows, 128), F32),
        vm((h, half, 2 * hid), F32), vm((h, half, 2 * hid), BF), vm((h, half, 2 * hid), BF),
        vm((h, 8, piece, 2 * hid), BF), vm((h, 4, piece, 2 * hid), BF), vm((h, 4, piece, 2 * hid), BF),
        vm((h, half, hid), F32), vm((h, half, hid), BF), vm((h, half, hid), BF),
        vm((h, 8, piece, hid), BF), vm((h, 4, piece, hid), BF), vm((h, 4, piece, hid), BF),
        vm((h, piece, 2 * hid), F32),
        vm((h, 2, ny, piece, hid), BF), vm((h, 2, ny, piece, 2 * hid), BF),
        vm((h, rows, 256), BF),
        along_x, along_z, along_x, along_z,
        vm((2, nz, rows_of, 256), BF), vm((2, nx, rows_of, 256), BF),
        vm((2, nz, rows_of, 256), BF), vm((2, nx, rows_of, 256), BF),
        dma((4, n)), dma((4, n)), dma((2, 2, h, n)), dma((2, 2, h, n)), dma((2 * h,)), dma((2 * h,)),
        dma((2 * h, 4)), dma((2 * h, 4)), dma((2 * h, 4)), dma((2 * h, 4)),
        dma((2 * h, 8)), dma((2 * h, 8)), dma((2 * h, n)), dma((2 * h, n)),
        dma((2, 2, h, n)), dma((2, 2, h, n)), dma((2, 2, n)), dma((2, 2, n)),
    ]
    combined, d_tokens, grad = pl.pallas_call(
        kernel,
        out_shape=(
            jax.ShapeDtypeStruct((rows_of, span), BF),
            jax.ShapeDtypeStruct((rows_of, span), BF),
            jax.ShapeDtypeStruct((span, 2, hid), BF),
        ),
        in_specs=[pl.BlockSpec(memory_space=pltpu.VMEM)] * 6,
        out_specs=[pl.BlockSpec(memory_space=pltpu.VMEM)] * 3,
        scratch_shapes=scratch,
        compiler_params=pltpu.CompilerParams(
            collective_id=0, has_side_effects=True, vmem_limit_bytes=48 * 2**20
        ),
        name="expert_layer",
    )(tokens, cotangent, routes.T, probs.T, w_gate_up.reshape(span, 2 * hid), w_down[0].T)
    return combined, d_tokens, grad[None]


def solution(mesh):
    placed = (
        P("expert", "dp"),
        P("expert", None),
        P("expert", None),
        P("expert", "dp"),
        P("expert", "dp", None, None),
        P("expert", None, "dp"),
    )
    return jax.shard_map(
        shards,
        mesh=mesh,
        in_specs=placed,
        out_specs=(P("expert", "dp"), P("expert", "dp"), P("expert", "dp", None, None)),
        check_vma=False,
    )
```
